32 devices in a mesh: seq: 8 (over z, y), chan: 4 (over x, core).
Axes of the slice: x: 2, y: 2, z: 4, core: 2. Of those that a mesh axis runs over, the one named last changes fastest.
Arguments:
- inputs: bfloat16 [2, 8192, 2048], P(None, 'seq', 'chan'), may hold values from -6 to 6
- mix_first: bfloat16 [32, 256, 256], P('seq'), may hold values from -0.375 to 0.375
- mix_second: bfloat16 [256, 32, 32], P('seq'), may hold values from -1 to 1
- gate_scale: float32 [2048], P('chan'), may hold values from 0.5 to 2
- gate_bias: float32 [2048], P('chan'), may hold values from -3 to 3
- up_first: bfloat16 [4, 512, 512], P('chan'), may hold values from -0.25 to 0.25
- up_second: bfloat16 [4, 2048, 512], P('chan'), may hold values from -0.25 to 0.25
- down_first: bfloat16 [4, 512, 2048], P('chan'), may hold values from -0.125 to 0.125
- down_second: bfloat16 [4, 512, 512], P('chan'), may hold values from -0.25 to 0.25
Outputs:
- layer_out: bfloat16 [2, 8192, 2048], P(None, ('seq', 'chan'))
The draws below stay inside these ranges and needn't reach their ends.
All inputs are finite; a program needn't handle non-finite values.
Results may differ from the reference program's by a relative error of at most 0.008.
Values may be sent and summed in bfloat16 or wider, within the bound.
A program may use at most 128 MiB of HBM per device.

```python
import math
import jax
import jax.numpy as jnp
from jax import lax

D = 2048
BLK = 256
SEQS = 2
NC = 4
NA = 32
LEN = 8192
CB = 512
HB = 2048


def block_scale(key, shape, split, low, largest):
    gain, own = 1.0, jax.random.fold_in(key, 6)
    for position, shards_of in split:
        steps = jnp.exp(jax.random.uniform(jax.random.fold_in(own, position), (shards_of,), jnp.float32, low / len(split), largest / len(split)))
        gain = gain * jnp.repeat(steps, shape[position] // shards_of).reshape([-1 if axis == position else 1 for axis in range(len(shape))])
    return gain


def bell_draw(stream_key, dims, width, limit, cuts=(), dtype=jnp.bfloat16):
    factor_of = block_scale(stream_key, dims, cuts, -0.22, 0.18) if cuts else 1.0
    entries = jax.random.normal(stream_key, dims, jnp.float32) * width * factor_of
    return jnp.minimum(jnp.maximum(entries, -limit), limit).astype(dtype)


def setup_inputs(seed: int = 0) -> dict:
    key_list = jax.random.split(jax.random.key(seed), 10)
    return {
        "inputs": bell_draw(key_list[0], (SEQS, LEN, D), 1.0, 6.0, ((1, 8), (2, 4))),
        "mix_first": bell_draw(key_list[1], (NA, BLK, BLK), BLK ** -0.5, 0.375, ((0, 8),)),
        "mix_second": bell_draw(key_list[2], (BLK, NA, NA), NA ** -0.5, 1.0, ((0, 8),)),
        "gate_scale": jnp.clip(jnp.exp(math.log(2.0) - 1.3862944 * jax.random.uniform(key_list[3], (D,), jnp.float32) ** block_scale(key_list[3], (D,), ((0, 4),), -0.2, 0.2)), 0.5, 2.0),
        "gate_bias": bell_draw(key_list[4], (D,), 1.0, 3.0, ((0, 4),), jnp.float32),
        "up_first": bell_draw(key_list[5], (NC, CB, CB), CB ** -0.5, 0.25, ((0, 4),)),
        "up_second": bell_draw(key_list[6], (NC, HB, CB), CB ** -0.5, 0.25, ((0, 4),)),
        "down_first": bell_draw(key_list[7], (NC, CB, HB), HB ** -0.5, 0.125, ((0, 4),)),
        "down_second": bell_draw(key_list[8], (NC, CB, CB), CB ** -0.5, 0.25, ((0, 4),)),
    }


def monarch(values, inner_weight, outer_weight):
    block_count = inner_weight.shape[0]
    inner_width = inner_weight.shape[1]
    in_width = inner_weight.shape[2]
    out_width = outer_weight.shape[1]
    leading = values.shape[:-1]
    blocked = values.reshape(leading + (block_count, in_width)).astype(jnp.float32)
    inner_rows = jnp.einsum('cqp,...cp->...cq', inner_weight.astype(jnp.float32), blocked).astype(jnp.bfloat16)
    permuted = jnp.swapaxes(inner_rows, -1, -2).reshape(leading + (block_count, inner_width)).astype(jnp.float32)
    projected = jnp.einsum('lor,...lr->...lo', outer_weight.astype(jnp.float32), permuted)
    return projected.reshape(leading + (block_count * out_width,))


def reference(inputs, mix_first, mix_second, gate_scale, gate_bias, up_first, up_second, down_first, down_second):
    def one_sequence(tokens):
        grouped = tokens.reshape(NA, BLK, D).astype(jnp.float32)
        first_pass = jnp.einsum('abq,aqd->abd', mix_first.astype(jnp.float32), grouped).astype(jnp.bfloat16)
        mixed_rows = jnp.einsum('bxy,ybd->xbd', mix_second.astype(jnp.float32), first_pass.astype(jnp.float32))
        mixed_rows = mixed_rows.astype(jnp.bfloat16).reshape(LEN, D).astype(jnp.float32)
        residual_in = tokens.astype(jnp.float32)
        hidden = (residual_in + mixed_rows * jax.nn.sigmoid(gate_scale * residual_in + gate_bias)).astype(jnp.bfloat16)
        expanded = monarch(hidden, up_first, up_second)
        activated = jax.nn.gelu(expanded, approximate=True).astype(jnp.bfloat16)
        contracted = monarch(activated, down_first, down_second)
        return (hidden.astype(jnp.float32) + contracted).astype(jnp.bfloat16)

    return lax.map(one_sequence, inputs)
```

```python
import functools

import jax
import jax.numpy as jnp
from jax import lax
from jax.experimental import pallas as pl
from jax.experimental.pallas import tpu as pltpu
from jax.sharding import PartitionSpec as P

MESH = pl.DeviceIdType.MESH
ROWS = 16


def shard_monarch(values, inner_weight, outer_weight):
    chan_count = lax.axis_size("chan")
    inner_width = inner_weight.shape[1]
    out_width = outer_weight.shape[1]
    sub_width = inner_width // chan_count
    seq_count, row_count = (values.shape[0], values.shape[1])
    inner_rows = jnp.einsum(
        "qp,stp->stq", inner_weight[0], values, preferred_element_type=jnp.float32
    )
    inner_rows = inner_rows.astype(jnp.bfloat16).reshape(
        seq_count, row_count, chan_count, sub_width
    )
    permuted = lax.all_to_all(inner_rows, "chan", split_axis=2, concat_axis=2, tiled=True)
    outer_blocks = outer_weight[0].reshape(out_width, sub_width, chan_count)
    return jnp.einsum("oqc,stcq->sto", outer_blocks, permuted, preferred_element_type=jnp.float32)


def dot(a, b):
    return jnp.dot(a, b, preferred_element_type=jnp.float32)


def dot_t(a, b):
    return lax.dot_general(a, b, (((1,), (1,)), ((), ())), preferred_element_type=jnp.float32)


def layer_kernel(
    n_seq,
    n_chan,
    x_ref,
    mix1_ref,
    mix2_ref,
    scale_ref,
    bias_ref,
    up1_ref,
    up2_ref,
    down1_ref,
    down2_ref,
    out_ref,
    first,
    gathered,
    second,
    mixed,
    hidden,
    inner1,
    perm1,
    inner2,
    perm2,
    result,
    up2p,
    down2p,
    spread,
    acc,
    fwd_send,
    fwd_recv,
    ret_send,
    ret_recv,
    c1_send,
    c1_recv,
    c2_send,
    c2_recv,
    out_send,
    out_recv,
    out_local,
):
    seqs, blocks, group, width = x_ref.shape
    na = n_seq * blocks
    own_b = group // n_seq
    sub = width // n_chan
    units = seqs * blocks
    me_s = lax.axis_index("seq")
    me_c = lax.axis_index("chan")

    barrier = pltpu.get_barrier_semaphore()
    for i in range(1, n_seq):
        pl.semaphore_signal(
            barrier, inc=1, device_id={"seq": lax.rem(me_s + i, n_seq)}, device_id_type=MESH
        )
    for i in range(1, n_chan):
        pl.semaphore_signal(
            barrier, inc=1, device_id={"chan": lax.rem(me_c + i, n_chan)}, device_id_type=MESH
        )
    pl.semaphore_wait(barrier, n_seq + n_chan - 2)

    my_b = pl.ds(pl.multiple_of(me_s * own_b, own_b), own_b)
    my_a = pl.ds(me_s * blocks, blocks)
    my_sub = pl.ds(pl.multiple_of(me_c * sub, sub), sub)
    my_cols = pl.ds(pl.multiple_of(me_c * width, width), width)

    def unit_of(k):
        j = lax.rem(k, blocks)
        half = blocks // 2
        return lax.div(k, blocks), lax.rem(j, 2) * half + lax.div(j, 2)

    @pl.loop(0, seqs)
    def _(s):
        @pl.loop(0, blocks)
        def _(a):
            first[s, a] = dot(mix1_ref[a], x_ref[s, a]).astype(jnp.bfloat16)

        @pl.loop(1, n_seq)
        def _(i):
            other = lax.rem(me_s + i, n_seq)
            rows = pl.ds(pl.multiple_of(other * own_b, own_b), own_b)
            pltpu.make_async_remote_copy(
                src_ref=first.at[s, :, rows, :],
                dst_ref=gathered.at[s, my_a],
                send_sem=fwd_send.at[s],
                recv_sem=fwd_recv.at[s],
                device_id={"seq": other},
                device_id_type=MESH,
            ).start()

        gathered[s, my_a] = first[s, :, my_b, :]

    span = na * ROWS
    row = lax.broadcasted_iota(jnp.int32, (width, width), 0)
    col = lax.broadcasted_iota(jnp.int32, (width, width), 1)
    order = (col == (row % sub) * n_chan + row // sub).astype(jnp.float32).astype(jnp.bfloat16)

    @pl.loop(0, up2_ref.shape[0] // width)
    def _(t):
        rows = pl.ds(pl.multiple_of(t * width, width), width)
        up2p[rows, :] = dot_t(up2_ref[rows, :], order).astype(jnp.bfloat16)

    down2p[...] = dot_t(down2_ref[...], order).astype(jnp.bfloat16)

    e_row = lax.broadcasted_iota(jnp.int32, (na, span), 0)
    e_col = lax.broadcasted_iota(jnp.int32, (na, span), 1)
    expand = (e_col // ROWS == e_row).astype(jnp.float32).astype(jnp.bfloat16)
    s_row = lax.broadcasted_iota(jnp.int32, (span, span), 0)
    s_col = lax.broadcasted_iota(jnp.int32, (span, span), 1)

    @pl.loop(0, own_b // ROWS)
    def _(g):
        wide = dot(mix2_ref[g], expand)
        spread[g] = jnp.where(s_row % ROWS == s_col % ROWS, wide, 0.0).astype(jnp.bfloat16)

    @pl.loop(0, seqs)
    def _(s):
        others = gathered.at[s, pl.ds(0, na - blocks)]
        pltpu.make_async_copy(others, others, fwd_recv.at[s]).wait()
        for g in range(own_b // ROWS):
            part = gathered[s, :, g * ROWS : (g + 1) * ROWS, :].reshape(span, width)
            got = dot(spread[g], part).astype(jnp.bfloat16)
            second[s, :, g * ROWS : (g + 1) * ROWS, :] = got.reshape(na, ROWS, width)

        @pl.loop(0, blocks)
        def _(j):
            k = s * blocks + j
            _, a = unit_of(k)

            @pl.loop(1, n_seq)
            def _(i):
                other = lax.rem(me_s + i, n_seq)
                pltpu.make_async_remote_copy(
                    src_ref=second.at[s, other * blocks + a],
                    dst_ref=mixed.at[k, my_b, :],
                    send_sem=ret_send.at[s],
                    recv_sem=ret_recv.at[k],
                    device_id={"seq": other},
                    device_id_type=MESH,
                ).start()

            mixed[k, my_b, :] = second[s, me_s * blocks + a]

    def swap(k, src, dst, send_sem, recv_sem):
        @pl.loop(1, n_chan)
        def _(i):
            other = lax.rem(me_c + i, n_chan)
            cols = pl.ds(pl.multiple_of(other * sub, sub), sub)
            pltpu.make_async_remote_copy(
                src_ref=src.at[k, :, cols],
                dst_ref=dst.at[k, :, my_sub],
                send_sem=send_sem.at[k],
                recv_sem=recv_sem.at[k],
                device_id={"chan": other},
                device_id_type=MESH,
            ).start()

        dst[k, :, my_sub] = src[k, :, my_sub]

    def await_swap(k, dst, sem):
        others = dst.at[k, :, pl.ds(0, width - sub)]
        pltpu.make_async_copy(others, others, sem.at[k]).wait()

    @pl.loop(0, units + 2)
    def _(step):
        @pl.when(step < units)
        def _():
            k = step
            s, a = unit_of(k)
            others = mixed.at[k, pl.ds(0, group - own_b), :]
            pltpu.make_async_copy(others, others, ret_recv.at[k]).wait()
            x = x_ref[s, a].astype(jnp.float32)
            gate = jax.nn.sigmoid(scale_ref[...] * x + bias_ref[...])
            hidden[k] = (x + mixed[k].astype(jnp.float32) * gate).astype(jnp.bfloat16)
            inner1[k] = dot_t(hidden[k], up1_ref[...]).astype(jnp.bfloat16)
            swap(k, inner1, perm1, c1_send, c1_recv)

        @pl.when((step >= 1) & (step < units + 1))
        def _():
            k = step - 1
            await_swap(k, perm1, c1_recv)
            acc[...] = jnp.zeros_like(acc)

            @pl.loop(0, up2_ref.shape[0] // width)
            def _(t):
                tile = pl.ds(pl.multiple_of(t * width, width), width)
                act = jax.nn.gelu(dot_t(perm1[k], up2p[tile, :]), approximate=True)
                acc[...] += dot_t(act.astype(jnp.bfloat16), down1_ref[:, tile])

            inner2[k] = acc[...].astype(jnp.bfloat16)
            swap(k, inner2, perm2, c2_send, c2_recv)

        @pl.when(step >= 2)
        def _():
            k = step - 2
            s, a = unit_of(k)
            await_swap(k, perm2, c2_recv)
            got = dot_t(perm2[k], down2p[...])
            result[k] = (hidden[k].astype(jnp.float32) + got).astype(jnp.bfloat16)

            @pl.when(a == me_c)
            def _():
                pltpu.make_async_copy(
                    result.at[k], out_ref.at[s, :, my_cols], out_local.at[s]
                ).start()

            @pl.when(a != me_c)
            def _():
                pltpu.make_async_remote_copy(
                    src_ref=result.at[k],
                    dst_ref=out_ref.at[s, :, my_cols],
                    send_sem=out_send.at[s],
                    recv_sem=out_recv.at[s],
                    device_id={"chan": a},
                    device_id_type=MESH,
                ).start()

    @pl.loop(0, seqs)
    def _(s):
        sent = gathered.at[s, pl.ds(0, na - blocks)]
        pltpu.make_async_copy(sent, sent, fwd_send.at[s]).wait()
        pltpu.make_async_copy(sent, sent, ret_send.at[s]).wait()
        landed = out_ref.at[s, :, pl.ds(0, width * (n_chan - 1))]
        pltpu.make_async_copy(landed, landed, out_send.at[s]).wait()
        pltpu.make_async_copy(landed, landed, out_recv.at[s]).wait()
        one = out_ref.at[s, :, pl.ds(0, width)]
        pltpu.make_async_copy(one, one, out_local.at[s]).wait()

    @pl.loop(0, units)
    def _(k):
        await_swap(k, perm1, c1_send)
        await_swap(k, perm2, c2_send)


def fused_layer(
    inputs,
    mix_first,
    mix_second,
    gate_scale,
    gate_bias,
    up_first,
    up_second,
    down_first,
    down_second,
):
    n_seq, n_chan = lax.axis_size("seq"), lax.axis_size("chan")
    seqs, rows, width = inputs.shape
    blocks, group = mix_first.shape[0], mix_first.shape[1]
    own_b, na = mix_second.shape[0], mix_second.shape[1]
    parts = own_b // ROWS
    units = seqs * blocks
    by_row = jnp.swapaxes(mix_second.reshape(parts, ROWS, na, na), 1, 2)
    bf = jnp.bfloat16
    per_unit = pltpu.VMEM((units, group, width), bf)
    per_b = pltpu.VMEM((seqs, na, own_b, width), bf)
    dma = pltpu.SemaphoreType.DMA
    return pl.pallas_call(
        functools.partial(layer_kernel, n_seq, n_chan),
        out_shape=jax.ShapeDtypeStruct((seqs, rows // n_chan, width * n_chan), bf),
        in_specs=[pl.BlockSpec(memory_space=pltpu.VMEM)] * 9,
        out_specs=pl.BlockSpec(memory_space=pl.ANY),
        scratch_shapes=[
            pltpu.VMEM((seqs, blocks, group, width), bf),
            per_b,
            per_b,
            per_unit,
            per_unit,
            per_unit,
            per_unit,
            per_unit,
            per_unit,
            per_unit,
            pltpu.VMEM(up_second.shape[1:], bf),
            pltpu.VMEM(down_second.shape[1:], bf),
            pltpu.VMEM((parts, na * ROWS, na * ROWS), bf),
            pltpu.VMEM((group, width), jnp.float32),
            dma((seqs,)),
            dma((seqs,)),
            dma((seqs,)),
            dma((units,)),
            dma((units,)),
            dma((units,)),
            dma((units,)),
            dma((units,)),
            dma((seqs,)),
            dma((seqs,)),
            dma((seqs,)),
        ],
        compiler_params=pltpu.CompilerParams(
            collective_id=0, has_side_effects=True, vmem_limit_bytes=56 * 1024 * 1024
        ),
    )(
        inputs.reshape(seqs, blocks, group, width),
        mix_first,
        by_row.reshape(parts, na * ROWS, na),
        gate_scale.reshape(1, width),
        gate_bias.reshape(1, width),
        up_first[0],
        up_second[0],
        down_first[0],
        down_second[0],
    )


def on_device(inputs, mix_first, mix_second, *rest):
    fits = mix_second.shape[0] % ROWS == 0 and mix_first.shape[0] == lax.axis_size("chan")
    run = fused_layer if fits else plain_layer
    return run(inputs, mix_first, mix_second, *rest)


def plain_layer(
    inputs,
    mix_first,
    mix_second,
    gate_scale,
    gate_bias,
    up_first,
    up_second,
    down_first,
    down_second,
):
    seq_count, row_count, chan_width = inputs.shape
    blocks_here = mix_first.shape[0]
    group_width = mix_first.shape[1]
    grouped = inputs.reshape(seq_count, blocks_here, group_width, chan_width)
    first_pass = jnp.einsum(
        "abq,saqc->sabc", mix_first, grouped, preferred_element_type=jnp.float32
    ).astype(jnp.bfloat16)
    mixed_rows = jnp.einsum(
        "bxy,sybc->sxbc",
        mix_second,
        lax.all_to_all(first_pass, "seq", split_axis=2, concat_axis=1, tiled=True),
        preferred_element_type=jnp.float32,
    ).astype(jnp.bfloat16)
    restored = lax.all_to_all(mixed_rows, "seq", split_axis=1, concat_axis=2, tiled=True).reshape(
        seq_count, row_count, chan_width
    )
    residual_in = inputs.astype(jnp.float32)
    hidden = (
        residual_in
        + restored.astype(jnp.float32) * jax.nn.sigmoid(gate_scale * residual_in + gate_bias)
    ).astype(jnp.bfloat16)
    expanded = shard_monarch(hidden, up_first, up_second)
    activated = jax.nn.gelu(expanded, approximate=True).astype(jnp.bfloat16)
    contracted = shard_monarch(activated, down_first, down_second)
    result = (hidden.astype(jnp.float32) + contracted).astype(jnp.bfloat16)
    return lax.all_to_all(result, "chan", split_axis=1, concat_axis=2, tiled=True)


def solution(mesh):
    return jax.shard_map(
        on_device,
        mesh=mesh,
        in_specs=(
            P(None, "seq", "chan"),
            P("seq", None, None),
            P("seq", None, None),
            P("chan"),
            P("chan"),
            P("chan", None, None),
            P("chan", None, None),
            P("chan", None, None),
            P("chan", None, None),
        ),
        out_specs=P(None, ("seq", "chan"), None),
        check_vma=False,
    )
```

```python
import functools

import jax
import jax.numpy as jnp
from jax import lax
from jax.experimental import pallas as pl
from jax.experimental.pallas import tpu as pltpu
from jax.sharding import PartitionSpec as P

MESH = pl.DeviceIdType.MESH
ROWS = 16
AHEAD = 2


def shard_monarch(values, inner_weight, outer_weight):
    chan_count = lax.axis_size("chan")
    inner_width = inner_weight.shape[1]
    out_width = outer_weight.shape[1]
    sub_width = inner_width // chan_count
    seq_count, row_count = (values.shape[0], values.shape[1])
    inner_rows = jnp.einsum(
        "qp,stp->stq", inner_weight[0], values, preferred_element_type=jnp.float32
    )
    inner_rows = inner_rows.astype(jnp.bfloat16).reshape(
        seq_count, row_count, chan_count, sub_width
    )
    permuted = lax.all_to_all(inner_rows, "chan", split_axis=2, concat_axis=2, tiled=True)
    outer_blocks = outer_weight[0].reshape(out_width, sub_width, chan_count)
    return jnp.einsum("oqc,stcq->sto", outer_blocks, permuted, preferred_element_type=jnp.float32)


def dot(a, b):
    return jnp.dot(a, b, preferred_element_type=jnp.float32)


def dot_t(a, b):
    return lax.dot_general(a, b, (((1,), (1,)), ((), ())), preferred_element_type=jnp.float32)


def layer_kernel(
    n_seq,
    n_chan,
    x_ref,
    mix1_ref,
    mix2_ref,
    scale_ref,
    bias_ref,
    up1_hbm,
    up2_hbm,
    down1_hbm,
    down2_hbm,
    out_ref,
    first,
    gathered,
    second,
    mixed,
    hidden,
    inner1,
    perm1,
    inner2,
    perm2,
    result,
    up2p,
    down2p,
    spread,
    acc,
    up1_ref,
    up2_ref,
    down1_ref,
    down2_ref,
    load_sem,
    fwd_send,
    fwd_recv,
    ret_send,
    ret_recv,
    c1_send,
    c1_recv,
    c2_send,
    c2_recv,
    out_send,
    out_recv,
    out_local,
):
    seqs, blocks, group, width = x_ref.shape
    na = n_seq * blocks
    own_b = group // n_seq
    sub = width // n_chan
    units = seqs * blocks
    me_s = lax.axis_index("seq")
    me_c = lax.axis_index("chan")

    barrier = pltpu.get_barrier_semaphore()
    for i in range(1, n_seq):
        pl.semaphore_signal(
            barrier, inc=1, device_id={"seq": lax.rem(me_s + i, n_seq)}, device_id_type=MESH
        )
    for i in range(1, n_chan):
        pl.semaphore_signal(
            barrier, inc=1, device_id={"chan": lax.rem(me_c + i, n_chan)}, device_id_type=MESH
        )

    loads = [
        pltpu.make_async_copy(src, dst, load_sem.at[i])
        for i, (src, dst) in enumerate(
            [(up2_hbm, up2_ref), (down2_hbm, down2_ref), (up1_hbm, up1_ref), (down1_hbm, down1_ref)]
        )
    ]
    for load in loads:
        load.start()

    my_b = pl.ds(pl.multiple_of(me_s * own_b, own_b), own_b)
    my_a = pl.ds(me_s * blocks, blocks)
    my_sub = pl.ds(pl.multiple_of(me_c * sub, sub), sub)
    my_cols = pl.ds(pl.multiple_of(me_c * width, width), width)

    def unit_of(k):
        j = lax.rem(k, blocks)
        half = blocks // 2
        return lax.div(k, blocks), lax.rem(j, 2) * half + lax.div(j, 2)

    parts = own_b // ROWS

    def run_first(s):
        @pl.loop(0, blocks)
        def _(a):
            first[s, a] = dot(mix1_ref[a], x_ref[s, a]).astype(jnp.bfloat16)

        gathered[s, my_a] = first[s, :, my_b, :]

    def send_first(s, g):
        landing = pl.ds(g * ROWS, ROWS)

        @pl.loop(1, n_seq)
        def _(i):
            other = lax.rem(me_s + i, n_seq)
            rows = pl.ds(pl.multiple_of(other * own_b + g * ROWS, ROWS), ROWS)
            pltpu.make_async_remote_copy(
                src_ref=first.at[s, :, rows, :],
                dst_ref=gathered.at[s, my_a, landing, :],
                send_sem=fwd_send.at[s * parts + g],
                recv_sem=fwd_recv.at[s * parts + g],
                device_id={"seq": other},
                device_id_type=MESH,
            ).start()

    def await_first(s, g, sem):
        others = gathered.at[s, pl.ds(0, na - blocks), pl.ds(g * ROWS, ROWS), :]
        pltpu.make_async_copy(others, others, sem.at[s * parts + g]).wait()

    run_first(0)
    pl.semaphore_wait(barrier, n_seq + n_chan - 2)
    for g in range(parts):
        send_first(0, g)

    @pl.loop(1, seqs)
    def _(s):
        run_first(s)

    for load in loads[:2]:
        load.wait()

    span = na * ROWS
    row = lax.broadcasted_iota(jnp.int32, (width, width), 0)
    col = lax.broadcasted_iota(jnp.int32, (width, width), 1)
    order = (col == (row % sub) * n_chan + row // sub).astype(jnp.float32).astype(jnp.bfloat16)

    @pl.loop(0, up2_ref.shape[0] // width)
    def _(t):
        rows = pl.ds(pl.multiple_of(t * width, width), width)
        up2p[rows, :] = dot_t(up2_ref[rows, :], order).astype(jnp.bfloat16)

    down2p[...] = dot_t(down2_ref[...], order).astype(jnp.bfloat16)

    e_row = lax.broadcasted_iota(jnp.int32, (na, span), 0)
    e_col = lax.broadcasted_iota(jnp.int32, (na, span), 1)
    expand = (e_col // ROWS == e_row).astype(jnp.float32).astype(jnp.bfloat16)
    s_row = lax.broadcasted_iota(jnp.int32, (span, span), 0)
    s_col = lax.broadcasted_iota(jnp.int32, (span, span), 1)

    @pl.loop(0, parts)
    def _(g):
        wide = dot(mix2_ref[g], expand)
        spread[g] = jnp.where(s_row % ROWS == s_col % ROWS, wide, 0.0).astype(jnp.bfloat16)

    for load in loads[2:]:
        load.wait()

    def run_second(s):
        for g in range(parts):
            rows = slice(g * ROWS, (g + 1) * ROWS)
            await_first(s, g, fwd_recv)
            if g == 0:

                @pl.when(s + 1 < seqs)
                def _():
                    send_first(s + 1, 0)

            part = gathered[s, :, rows, :].reshape(span, width)
            got = dot(spread[g], part).astype(jnp.bfloat16)
            second[s, :, rows, :] = got.reshape(na, ROWS, width)

        @pl.loop(s * blocks, (s + 1) * blocks)
        def _(k):
            _, a = unit_of(k)
            mixed[k, my_b, :] = second[s, me_s * blocks + a]

    def send_second(k):
        s, a = unit_of(k)

        @pl.loop(1, n_seq)
        def _(i):
            other = lax.rem(me_s + i, n_seq)
            pltpu.make_async_remote_copy(
                src_ref=second.at[s, other * blocks + a],
                dst_ref=mixed.at[k, my_b, :],
                send_sem=ret_send.at[k],
                recv_sem=ret_recv.at[k],
                device_id={"seq": other},
                device_id_type=MESH,
            ).start()

    def await_second(k, sem):
        others = mixed.at[k, pl.ds(0, group - own_b), :]
        pltpu.make_async_copy(others, others, sem.at[k]).wait()

    def swap(k, src, dst, send_sem, recv_sem):
        @pl.loop(1, n_chan)
        def _(i):
            other = lax.rem(me_c + i, n_chan)
            cols = pl.ds(pl.multiple_of(other * sub, sub), sub)
            pltpu.make_async_remote_copy(
                src_ref=src.at[k, :, cols],
                dst_ref=dst.at[k, :, my_sub],
                send_sem=send_sem.at[k],
                recv_sem=recv_sem.at[k],
                device_id={"chan": other},
                device_id_type=MESH,
            ).start()

        dst[k, :, my_sub] = src[k, :, my_sub]

    def await_swap(k, dst, sem):
        others = dst.at[k, :, pl.ds(0, width - sub)]
        pltpu.make_async_copy(others, others, sem.at[k]).wait()

    @pl.loop(0, units + 2)
    def _(step):
        @pl.when(step < units)
        def _():
            k = step
            s, a = unit_of(k)
            j = lax.rem(k, blocks)

            @pl.when(j == 0)
            def _():
                run_second(s)

                @pl.loop(0, AHEAD)
                def _(i):
                    send_second(k + i)

            @pl.when(j + AHEAD < blocks)
            def _():
                send_second(k + AHEAD)

            @pl.when((j == 1) & (s + 1 < seqs))
            def _():
                for g in range(1, parts):
                    send_first(s + 1, g)

            await_second(k, ret_recv)
            x = x_ref[s, a].astype(jnp.float32)
            gate = jax.nn.sigmoid(scale_ref[...] * x + bias_ref[...])
            hidden[k] = (x + mixed[k].astype(jnp.float32) * gate).astype(jnp.bfloat16)
            inner1[k] = dot_t(hidden[k], up1_ref[...]).astype(jnp.bfloat16)
            swap(k, inner1, perm1, c1_send, c1_recv)

        @pl.when((step >= 1) & (step < units + 1))
        def _():
            k = step - 1
            await_swap(k, perm1, c1_recv)
            acc[...] = jnp.zeros_like(acc)

            @pl.loop(0, up2_ref.shape[0] // width)
            def _(t):
                tile = pl.ds(pl.multiple_of(t * width, width), width)
                act = jax.nn.gelu(dot_t(perm1[k], up2p[tile, :]), approximate=True)
                acc[...] += dot_t(act.astype(jnp.bfloat16), down1_ref[:, tile])

            inner2[k] = acc[...].astype(jnp.bfloat16)
            swap(k, inner2, perm2, c2_send, c2_recv)

        @pl.when(step >= 2)
        def _():
            k = step - 2
            s, a = unit_of(k)
            await_swap(k, perm2, c2_recv)
            got = dot_t(perm2[k], down2p[...])
            result[k] = (hidden[k].astype(jnp.float32) + got).astype(jnp.bfloat16)

            @pl.when(a == me_c)
            def _():
                pltpu.make_async_copy(
                    result.at[k], out_ref.at[s, :, my_cols], out_local.at[s]
                ).start()

            @pl.when(a != me_c)
            def _():
                pltpu.make_async_remote_copy(
                    src_ref=result.at[k],
                    dst_ref=out_ref.at[s, :, my_cols],
                    send_sem=out_send.at[s],
                    recv_sem=out_recv.at[s],
                    device_id={"chan": a},
                    device_id_type=MESH,
                ).start()

    @pl.loop(0, seqs)
    def _(s):
        for g in range(parts):
            await_first(s, g, fwd_send)
        landed = out_ref.at[s, :, pl.ds(0, width * (n_chan - 1))]
        pltpu.make_async_copy(landed, landed, out_send.at[s]).wait()
        pltpu.make_async_copy(landed, landed, out_recv.at[s]).wait()
        one = out_ref.at[s, :, pl.ds(0, width)]
        pltpu.make_async_copy(one, one, out_local.at[s]).wait()

    @pl.loop(0, units)
    def _(k):
        await_second(k, ret_send)
        await_swap(k, perm1, c1_send)
        await_swap(k, perm2, c2_send)


def fused_layer(
    inputs,
    mix_first,
    mix_second,
    gate_scale,
    gate_bias,
    up_first,
    up_second,
    down_first,
    down_second,
):
    n_seq, n_chan = lax.axis_size("seq"), lax.axis_size("chan")
    seqs, rows, width = inputs.shape
    blocks, group = mix_first.shape[0], mix_first.shape[1]
    own_b, na = mix_second.shape[0], mix_second.shape[1]
    parts = own_b // ROWS
    units = seqs * blocks
    by_row = jnp.swapaxes(mix_second.reshape(parts, ROWS, na, na), 1, 2)
    bf = jnp.bfloat16
    per_unit = pltpu.VMEM((units, group, width), bf)
    per_b = pltpu.VMEM((seqs, na, own_b, width), bf)
    dma = pltpu.SemaphoreType.DMA
    return pl.pallas_call(
        functools.partial(layer_kernel, n_seq, n_chan),
        out_shape=jax.ShapeDtypeStruct((seqs, rows // n_chan, width * n_chan), bf),
        in_specs=[pl.BlockSpec(memory_space=pltpu.VMEM)] * 5
        + [pl.BlockSpec(memory_space=pl.ANY)] * 4,
        out_specs=pl.BlockSpec(memory_space=pl.ANY),
        scratch_shapes=[
            pltpu.VMEM((seqs, blocks, group, width), bf),
            per_b,
            per_b,
            per_unit,
            per_unit,
            per_unit,
            per_unit,
            per_unit,
            per_unit,
            per_unit,
            pltpu.VMEM(up_second.shape[1:], bf),
            pltpu.VMEM(down_second.shape[1:], bf),
            pltpu.VMEM((parts, na * ROWS, na * ROWS), bf),
            pltpu.VMEM((group, width), jnp.float32),
            pltpu.VMEM(up_first.shape[1:], bf),
            pltpu.VMEM(up_second.shape[1:], bf),
            pltpu.VMEM(down_first.shape[1:], bf),
            pltpu.VMEM(down_second.shape[1:], bf),
            dma((4,)),
            dma((seqs * parts,)),
            dma((seqs * parts,)),
            dma((units,)),
            dma((units,)),
            dma((units,)),
            dma((units,)),
            dma((units,)),
            dma((units,)),
            dma((seqs,)),
            dma((seqs,)),
            dma((seqs,)),
        ],
        compiler_params=pltpu.CompilerParams(
            collective_id=0, has_side_effects=True, vmem_limit_bytes=56 * 1024 * 1024
        ),
    )(
        inputs.reshape(seqs, blocks, group, width),
        mix_first,
        by_row.reshape(parts, na * ROWS, na),
        gate_scale.reshape(1, width),
        gate_bias.reshape(1, width),
        up_first[0],
        up_second[0],
        down_first[0],
        down_second[0],
    )


def on_device(inputs, mix_first, mix_second, *rest):
    fits = mix_second.shape[0] % ROWS == 0 and mix_first.shape[0] == lax.axis_size("chan")
    run = fused_layer if fits else plain_layer
    return run(inputs, mix_first, mix_second, *rest)


def plain_layer(
    inputs,
    mix_first,
    mix_second,
    gate_scale,
    gate_bias,
    up_first,
    up_second,
    down_first,
    down_second,
):
    seq_count, row_count, chan_width = inputs.shape
    blocks_here = mix_first.shape[0]
    group_width = mix_first.shape[1]
    grouped = inputs.reshape(seq_count, blocks_here, group_width, chan_width)
    first_pass = jnp.einsum(
        "abq,saqc->sabc", mix_first, grouped, preferred_element_type=jnp.float32
    ).astype(jnp.bfloat16)
    mixed_rows = jnp.einsum(
        "bxy,sybc->sxbc",
        mix_second,
        lax.all_to_all(first_pass, "seq", split_axis=2, concat_axis=1, tiled=True),
        preferred_element_type=jnp.float32,
    ).astype(jnp.bfloat16)
    restored = lax.all_to_all(mixed_rows, "seq", split_axis=1, concat_axis=2, tiled=True).reshape(
        seq_count, row_count, chan_width
    )
    residual_in = inputs.astype(jnp.float32)
    hidden = (
        residual_in
        + restored.astype(jnp.float32) * jax.nn.sigmoid(gate_scale * residual_in + gate_bias)
    ).astype(jnp.bfloat16)
    expanded = shard_monarch(hidden, up_first, up_second)
    activated = jax.nn.gelu(expanded, approximate=True).astype(jnp.bfloat16)
    contracted = shard_monarch(activated, down_first, down_second)
    result = (hidden.astype(jnp.float32) + contracted).astype(jnp.bfloat16)
    return lax.all_to_all(result, "chan", split_axis=1, concat_axis=2, tiled=True)


def solution(mesh):
    return jax.shard_map(
        on_device,
        mesh=mesh,
        in_specs=(
            P(None, "seq", "chan"),
            P("seq", None, None),
            P("seq", None, None),
            P("chan"),
            P("chan"),
            P("chan", None, None),
            P("chan", None, None),
            P("chan", None, None),
            P("chan", None, None),
        ),
        out_specs=P(None, ("seq", "chan"), None),
        check_vma=False,
    )
```

```python
import functools

import jax
import jax.numpy as jnp
from jax import lax
from jax.experimental import pallas as pl
from jax.experimental.pallas import tpu as pltpu
from jax.sharding import PartitionSpec as P

MESH = pl.DeviceIdType.MESH
ROWS = 16
LANES = 2
AHEAD = 2


def shard_monarch(values, inner_weight, outer_weight):
    chan_count = lax.axis_size("chan")
    inner_width = inner_weight.shape[1]
    out_width = outer_weight.shape[1]
    sub_width = inner_width // chan_count
    seq_count, row_count = (values.shape[0], values.shape[1])
    inner_rows = jnp.einsum(
        "qp,stp->stq", inner_weight[0], values, preferred_element_type=jnp.float32
    )
    inner_rows = inner_rows.astype(jnp.bfloat16).reshape(
        seq_count, row_count, chan_count, sub_width
    )
    permuted = lax.all_to_all(inner_rows, "chan", split_axis=2, concat_axis=2, tiled=True)
    outer_blocks = outer_weight[0].reshape(out_width, sub_width, chan_count)
    return jnp.einsum("oqc,stcq->sto", outer_blocks, permuted, preferred_element_type=jnp.float32)


def dot(a, b):
    return jnp.dot(a, b, preferred_element_type=jnp.float32)


def dot_t(a, b):
    return lax.dot_general(a, b, (((1,), (1,)), ((), ())), preferred_element_type=jnp.float32)


def layer_kernel(
    n_seq,
    n_chan,
    x_ref,
    mix1_ref,
    mix2_ref,
    scale_ref,
    bias_ref,
    up1_hbm,
    up2_hbm,
    down1_hbm,
    down2_hbm,
    out_ref,
    first,
    gathered,
    second,
    mixed,
    hidden,
    inner1,
    perm1,
    inner2,
    perm2,
    result,
    up2p,
    down2p,
    spread,
    acc,
    up1_ref,
    up2_ref,
    down1_ref,
    down2_ref,
    load_sem,
    fwd_send,
    fwd_recv,
    ret_send,
    ret_recv,
    c1_send,
    c1_recv,
    c2_send,
    c2_recv,
    out_send,
    out_recv,
    out_local,
):
    seqs, blocks, _, parts, _, width = x_ref.shape
    na = n_seq * blocks
    group = n_seq * parts * ROWS
    sub = width // n_chan
    chunks = seqs * parts
    units = chunks * LANES
    paired = blocks // LANES
    half = n_seq * ROWS
    me_s = lax.axis_index("seq")
    me_c = lax.axis_index("chan")

    barrier = pltpu.get_barrier_semaphore()
    for i in range(1, n_seq):
        pl.semaphore_signal(
            barrier, inc=1, device_id={"seq": lax.rem(me_s + i, n_seq)}, device_id_type=MESH
        )
    for i in range(1, n_chan):
        pl.semaphore_signal(
            barrier, inc=1, device_id={"chan": lax.rem(me_c + i, n_chan)}, device_id_type=MESH
        )

    loads = [
        pltpu.make_async_copy(src, dst, load_sem.at[i])
        for i, (src, dst) in enumerate(
            [(up2_hbm, up2_ref), (down2_hbm, down2_ref), (up1_hbm, up1_ref), (down1_hbm, down1_ref)]
        )
    ]
    for load in loads:
        load.start()

    my_a = pl.ds(me_s * blocks, blocks)
    my_sub = pl.ds(pl.multiple_of(me_c * sub, sub), sub)
    my_cols = pl.ds(pl.multiple_of(me_c * width, width), width)

    def run_first(s):
        @pl.loop(0, blocks)
        def _(a):
            got = dot(mix1_ref[a], x_ref[s, a].reshape(group, width)).astype(jnp.bfloat16)
            first[s, a] = got.reshape(n_seq, parts, ROWS, width)

        for g in range(parts):
            gathered[s * parts + g, my_a] = first[s, :, me_s, g]

    def send_first(q):
        @pl.loop(1, n_seq)
        def _(i):
            other = lax.rem(me_s + i, n_seq)
            pltpu.make_async_remote_copy(
                src_ref=first.at[lax.div(q, parts), :, other, lax.rem(q, parts)],
                dst_ref=gathered.at[q, my_a],
                send_sem=fwd_send.at[q],
                recv_sem=fwd_recv.at[q],
                device_id={"seq": other},
                device_id_type=MESH,
            ).start()

    def await_first(q, sem):
        others = gathered.at[q, pl.ds(0, na - blocks)]
        pltpu.make_async_copy(others, others, sem.at[q]).wait()

    run_first(0)
    pl.semaphore_wait(barrier, n_seq + n_chan - 2)
    for q in range(min(AHEAD, parts)):
        send_first(jnp.int32(q))

    @pl.loop(1, seqs)
    def _(s):
        run_first(s)

    for load in loads[:2]:
        load.wait()

    span = na * ROWS
    row = lax.broadcasted_iota(jnp.int32, (width, width), 0)
    col = lax.broadcasted_iota(jnp.int32, (width, width), 1)
    order = (col == (row % sub) * n_chan + row // sub).astype(jnp.float32).astype(jnp.bfloat16)

    @pl.loop(0, up2_ref.shape[0] // width)
    def _(t):
        rows = pl.ds(pl.multiple_of(t * width, width), width)
        up2p[rows, :] = dot_t(up2_ref[rows, :], order).astype(jnp.bfloat16)

    down2p[...] = dot_t(down2_ref[...], order).astype(jnp.bfloat16)

    e_row = lax.broadcasted_iota(jnp.int32, (na, span), 0)
    e_col = lax.broadcasted_iota(jnp.int32, (na, span), 1)
    expand = (e_col // ROWS == e_row).astype(jnp.float32).astype(jnp.bfloat16)
    s_row = lax.broadcasted_iota(jnp.int32, (span, span), 0)
    s_col = lax.broadcasted_iota(jnp.int32, (span, span), 1)

    @pl.loop(0, parts)
    def _(g):
        wide = dot(mix2_ref[g], expand)
        spread[g] = jnp.where(s_row % ROWS == s_col % ROWS, wide, 0.0).astype(jnp.bfloat16)

    for load in loads[2:]:
        load.wait()

    def run_second(q):
        await_first(q, fwd_recv)
        part = gathered[q].reshape(span, width)
        got = dot(spread[lax.rem(q, parts)], part).astype(jnp.bfloat16)
        second[q] = got.reshape(n_seq, paired, LANES, ROWS, width)

        @pl.loop(0, LANES)
        def _(lane):
            k = q * LANES + lane
            mixed[k, :, me_s] = second[q, me_s, :, lane]
            send_second(q, lane)

    def send_second(q, lane):
        k = q * LANES + lane

        @pl.loop(1, n_seq)
        def _(i):
            other = lax.rem(me_s + i, n_seq)
            pltpu.make_async_remote_copy(
                src_ref=second.at[q, other, :, lane],
                dst_ref=mixed.at[k, :, me_s],
                send_sem=ret_send.at[k],
                recv_sem=ret_recv.at[k],
                device_id={"seq": other},
                device_id_type=MESH,
            ).start()

    def await_second(k, sem):
        others = mixed.at[k, :, pl.ds(0, n_seq - 1)]
        pltpu.make_async_copy(others, others, sem.at[k]).wait()

    def swap(k, src, dst, send_sem, recv_sem):
        @pl.loop(1, n_chan)
        def _(i):
            other = lax.rem(me_c + i, n_chan)
            cols = pl.ds(pl.multiple_of(other * sub, sub), sub)
            pltpu.make_async_remote_copy(
                src_ref=src.at[k, :, cols],
                dst_ref=dst.at[k, :, my_sub],
                send_sem=send_sem.at[k],
                recv_sem=recv_sem.at[k],
                device_id={"chan": other},
                device_id_type=MESH,
            ).start()

        dst[k, :, my_sub] = src[k, :, my_sub]

    def await_swap(k, dst, sem):
        others = dst.at[k, :, pl.ds(0, width - sub)]
        pltpu.make_async_copy(others, others, sem.at[k]).wait()

    @pl.loop(0, units + 2)
    def _(step):
        @pl.when(step < units)
        def _():
            k = step
            q, lane = lax.div(k, LANES), lax.rem(k, LANES)
            s, g = lax.div(q, parts), lax.rem(q, parts)

            @pl.when(lane == 0)
            def _():
                run_second(q)

            @pl.when((lane == 1) & (q + AHEAD < chunks))
            def _():
                send_first(q + AHEAD)

            await_second(k, ret_recv)
            for pair in range(paired):
                x = x_ref[s, pair * LANES + lane, :, g].reshape(half, width).astype(jnp.float32)
                gate = jax.nn.sigmoid(scale_ref[...] * x + bias_ref[...])
                mix = mixed[k, pair].reshape(half, width).astype(jnp.float32)
                hidden[k, pair * half : (pair + 1) * half] = (x + mix * gate).astype(jnp.bfloat16)
            inner1[k] = dot_t(hidden[k], up1_ref[...]).astype(jnp.bfloat16)
            swap(k, inner1, perm1, c1_send, c1_recv)

        @pl.when((step >= 1) & (step < units + 1))
        def _():
            k = step - 1
            await_swap(k, perm1, c1_recv)
            acc[...] = jnp.zeros_like(acc)

            @pl.loop(0, up2_ref.shape[0] // width)
            def _(t):
                tile = pl.ds(pl.multiple_of(t * width, width), width)
                act = jax.nn.gelu(dot_t(perm1[k], up2p[tile, :]), approximate=True)
                acc[...] += dot_t(act.astype(jnp.bfloat16), down1_ref[:, tile])

            inner2[k] = acc[...].astype(jnp.bfloat16)
            swap(k, inner2, perm2, c2_send, c2_recv)

        @pl.when(step >= 2)
        def _():
            k = step - 2
            q, lane = lax.div(k, LANES), lax.rem(k, LANES)
            s, g = lax.div(q, parts), lax.rem(q, parts)
            await_swap(k, perm2, c2_recv)
            got = dot_t(perm2[k], down2p[...])
            got = (hidden[k].astype(jnp.float32) + got).astype(jnp.bfloat16)
            result[k] = got.reshape(paired, n_seq, ROWS, width)
            for pair in range(paired):
                a = pair * LANES + lane
                src, dst = result.at[k, pair], out_ref.at[s, :, g, :, my_cols]

                @pl.when(a == me_c)
                def _(src=src, dst=dst):
                    pltpu.make_async_copy(src, dst, out_local.at[s]).start()

                @pl.when(a != me_c)
                def _(src=src, dst=dst, a=a):
                    pltpu.make_async_remote_copy(
                        src_ref=src,
                        dst_ref=dst,
                        send_sem=out_send.at[s],
                        recv_sem=out_recv.at[s],
                        device_id={"chan": a},
                        device_id_type=MESH,
                    ).start()

    @pl.loop(0, seqs)
    def _(s):
        landed = out_ref.at[s, :, :, :, pl.ds(0, width * (n_chan - 1))]
        pltpu.make_async_copy(landed, landed, out_send.at[s]).wait()
        pltpu.make_async_copy(landed, landed, out_recv.at[s]).wait()
        one = out_ref.at[s, :, :, :, pl.ds(0, width)]
        pltpu.make_async_copy(one, one, out_local.at[s]).wait()

    @pl.loop(0, chunks)
    def _(q):
        await_first(q, fwd_send)

    @pl.loop(0, units)
    def _(k):
        await_second(k, ret_send)
        await_swap(k, perm1, c1_send)
        await_swap(k, perm2, c2_send)


def fused_layer(
    inputs,
    mix_first,
    mix_second,
    gate_scale,
    gate_bias,
    up_first,
    up_second,
    down_first,
    down_second,
):
    n_seq, n_chan = lax.axis_size("seq"), lax.axis_size("chan")
    seqs, rows, width = inputs.shape
    blocks, group = mix_first.shape[0], mix_first.shape[1]
    own_b, na = mix_second.shape[0], mix_second.shape[1]
    parts = own_b // ROWS
    chunks = seqs * parts
    units = chunks * LANES
    paired = blocks // LANES
    by_row = jnp.swapaxes(mix_second.reshape(parts, ROWS, na, na), 1, 2)
    bf = jnp.bfloat16
    per_unit = pltpu.VMEM((units, paired * n_seq * ROWS, width), bf)
    by_device = pltpu.VMEM((units, paired, n_seq, ROWS, width), bf)
    dma = pltpu.SemaphoreType.DMA
    out = pl.pallas_call(
        functools.partial(layer_kernel, n_seq, n_chan),
        out_shape=jax.ShapeDtypeStruct((seqs, n_seq, parts, ROWS, width * n_chan), bf),
        in_specs=[pl.BlockSpec(memory_space=pltpu.VMEM)] * 5
        + [pl.BlockSpec(memory_space=pl.ANY)] * 4,
        out_specs=pl.BlockSpec(memory_space=pl.ANY),
        scratch_shapes=[
            pltpu.VMEM((seqs, blocks, n_seq, parts, ROWS, width), bf),
            pltpu.VMEM((chunks, na, ROWS, width), bf),
            pltpu.VMEM((chunks, n_seq, paired, LANES, ROWS, width), bf),
            by_device,
            per_unit,
            per_unit,
            per_unit,
            per_unit,
            per_unit,
            by_device,
            pltpu.VMEM(up_second.shape[1:], bf),
            pltpu.VMEM(down_second.shape[1:], bf),
            pltpu.VMEM((parts, na * ROWS, na * ROWS), bf),
            pltpu.VMEM((paired * n_seq * ROWS, width), jnp.float32),
            pltpu.VMEM(up_first.shape[1:], bf),
            pltpu.VMEM(up_second.shape[1:], bf),
            pltpu.VMEM(down_first.shape[1:], bf),
            pltpu.VMEM(down_second.shape[1:], bf),
            dma((4,)),
            dma((chunks,)),
            dma((chunks,)),
            dma((units,)),
            dma((units,)),
            dma((units,)),
            dma((units,)),
            dma((units,)),
            dma((units,)),
            dma((seqs,)),
            dma((seqs,)),
            dma((seqs,)),
        ],
        compiler_params=pltpu.CompilerParams(
            collective_id=0, has_side_effects=True, vmem_limit_bytes=56 * 1024 * 1024
        ),
    )(
        inputs.reshape(seqs, blocks, n_seq, parts, ROWS, width),
        mix_first,
        by_row.reshape(parts, na * ROWS, na),
        gate_scale.reshape(1, width),
        gate_bias.reshape(1, width),
        up_first[0],
        up_second[0],
        down_first[0],
        down_second[0],
    )
    return out.reshape(seqs, group, width * n_chan)


def on_device(inputs, mix_first, mix_second, *rest):
    blocks = mix_first.shape[0]
    whole = mix_second.shape[0] % ROWS == 0 and blocks % LANES == 0
    fits = whole and blocks == lax.axis_size("chan")
    run = fused_layer if fits else plain_layer
    return run(inputs, mix_first, mix_second, *rest)


def plain_layer(
    inputs,
    mix_first,
    mix_second,
    gate_scale,
    gate_bias,
    up_first,
    up_second,
    down_first,
    down_second,
):
    seq_count, row_count, chan_width = inputs.shape
    blocks_here = mix_first.shape[0]
    group_width = mix_first.shape[1]
    grouped = inputs.reshape(seq_count, blocks_here, group_width, chan_width)
    first_pass = jnp.einsum(
        "abq,saqc->sabc", mix_first, grouped, preferred_element_type=jnp.float32
    ).astype(jnp.bfloat16)
    mixed_rows = jnp.einsum(
        "bxy,sybc->sxbc",
        mix_second,
        lax.all_to_all(first_pass, "seq", split_axis=2, concat_axis=1, tiled=True),
        preferred_element_type=jnp.float32,
    ).astype(jnp.bfloat16)
    restored = lax.all_to_all(mixed_rows, "seq", split_axis=1, concat_axis=2, tiled=True).reshape(
        seq_count, row_count, chan_width
    )
    residual_in = inputs.astype(jnp.float32)
    hidden = (
        residual_in
        + restored.astype(jnp.float32) * jax.nn.sigmoid(gate_scale * residual_in + gate_bias)
    ).astype(jnp.bfloat16)
    expanded = shard_monarch(hidden, up_first, up_second)
    activated = jax.nn.gelu(expanded, approximate=True).astype(jnp.bfloat16)
    contracted = shard_monarch(activated, down_first, down_second)
    result = (hidden.astype(jnp.float32) + contracted).astype(jnp.bfloat16)
    return lax.all_to_all(result, "chan", split_axis=1, concat_axis=2, tiled=True)


def solution(mesh):
    return jax.shard_map(
        on_device,
        mesh=mesh,
        in_specs=(
            P(None, "seq", "chan"),
            P("seq", None, None),
            P("seq", None, None),
            P("chan"),
            P("chan"),
            P("chan", None, None),
            P("chan", None, None),
            P("chan", None, None),
            P("chan", None, None),
        ),
        out_specs=P(None, ("seq", "chan"), None),
        check_vma=False,
    )
```

```python
import functools

import jax
import jax.numpy as jnp
from jax import lax
from jax.experimental import pallas as pl
from jax.experimental.pallas import tpu as pltpu
from jax.sharding import PartitionSpec as P

MESH = pl.DeviceIdType.MESH
ROWS = 16
LANES = 2
AHEAD = 2


def shard_monarch(values, inner_weight, outer_weight):
    chan_count = lax.axis_size("chan")
    inner_width = inner_weight.shape[1]
    out_width = outer_weight.shape[1]
    sub_width = inner_width // chan_count
    seq_count, row_count = (values.shape[0], values.shape[1])
    inner_rows = jnp.einsum(
        "qp,stp->stq", inner_weight[0], values, preferred_element_type=jnp.float32
    )
    inner_rows = inner_rows.astype(jnp.bfloat16).reshape(
        seq_count, row_count, chan_count, sub_width
    )
    permuted = lax.all_to_all(inner_rows, "chan", split_axis=2, concat_axis=2, tiled=True)
    outer_blocks = outer_weight[0].reshape(out_width, sub_width, chan_count)
    return jnp.einsum("oqc,stcq->sto", outer_blocks, permuted, preferred_element_type=jnp.float32)


def dot(a, b):
    return jnp.dot(a, b, preferred_element_type=jnp.float32)


def dot_t(a, b):
    return lax.dot_general(a, b, (((1,), (1,)), ((), ())), preferred_element_type=jnp.float32)


def layer_kernel(
    n_seq,
    n_chan,
    x_ref,
    mix1_ref,
    mix2_ref,
    scale_ref,
    bias_ref,
    up1_hbm,
    up2_hbm,
    down1_hbm,
    down2_hbm,
    out_ref,
    first,
    gathered,
    second,
    mixed,
    hidden,
    inner1,
    perm1,
    inner2,
    perm2,
    result,
    up2p,
    down2p,
    spread,
    acc,
    up1_ref,
    up2_ref,
    down1_ref,
    down2_ref,
    load_sem,
    fwd_send,
    fwd_recv,
    ret_send,
    ret_recv,
    c1_send,
    c1_recv,
    c2_send,
    c2_recv,
    out_send,
    out_recv,
    out_local,
):
    seqs, blocks, _, parts, _, width = x_ref.shape
    na = n_seq * blocks
    group = n_seq * parts * ROWS
    sub = width // n_chan
    chunks = seqs * parts
    units = chunks * LANES
    paired = blocks // LANES
    half = n_seq * ROWS
    me_s = lax.axis_index("seq")
    me_c = lax.axis_index("chan")

    barrier = pltpu.get_barrier_semaphore()
    for i in range(1, n_seq):
        pl.semaphore_signal(
            barrier, inc=1, device_id={"seq": lax.rem(me_s + i, n_seq)}, device_id_type=MESH
        )
    for i in range(1, n_chan):
        pl.semaphore_signal(
            barrier, inc=1, device_id={"chan": lax.rem(me_c + i, n_chan)}, device_id_type=MESH
        )

    loads = [
        pltpu.make_async_copy(src, dst, load_sem.at[i])
        for i, (src, dst) in enumerate(
            [(up2_hbm, up2_ref), (down2_hbm, down2_ref), (up1_hbm, up1_ref), (down1_hbm, down1_ref)]
        )
    ]
    for load in loads:
        load.start()

    my_a = pl.ds(me_s * blocks, blocks)
    my_sub = pl.ds(pl.multiple_of(me_c * sub, sub), sub)
    my_cols = pl.ds(pl.multiple_of(me_c * width, width), width)

    def run_first(s):
        @pl.loop(0, blocks)
        def _(a):
            got = dot(mix1_ref[a], x_ref[s, a].reshape(group, width)).astype(jnp.bfloat16)
            first[s, a] = got.reshape(n_seq, parts, ROWS, width)

        for g in range(parts):
            gathered[s * parts + g, my_a] = first[s, :, me_s, g]

    def send_first(q):
        @pl.loop(1, n_seq)
        def _(i):
            other = lax.rem(me_s + i, n_seq)
            pltpu.make_async_remote_copy(
                src_ref=first.at[lax.div(q, parts), :, other, lax.rem(q, parts)],
                dst_ref=gathered.at[q, my_a],
                send_sem=fwd_send.at[q],
                recv_sem=fwd_recv.at[q],
                device_id={"seq": other},
                device_id_type=MESH,
            ).start()

    def await_first(q, sem):
        others = gathered.at[q, pl.ds(0, na - blocks)]
        pltpu.make_async_copy(others, others, sem.at[q]).wait()

    run_first(0)
    pl.semaphore_wait(barrier, n_seq + n_chan - 2)
    for q in range(min(AHEAD, parts)):
        send_first(jnp.int32(q))

    @pl.loop(1, seqs)
    def _(s):
        run_first(s)

    for load in loads[:2]:
        load.wait()

    span = na * ROWS
    row = lax.broadcasted_iota(jnp.int32, (width, width), 0)
    col = lax.broadcasted_iota(jnp.int32, (width, width), 1)
    order = (col == (row % sub) * n_chan + row // sub).astype(jnp.float32).astype(jnp.bfloat16)

    @pl.loop(0, up2_ref.shape[0] // width)
    def _(t):
        rows = pl.ds(pl.multiple_of(t * width, width), width)
        up2p[rows, :] = dot_t(up2_ref[rows, :], order).astype(jnp.bfloat16)

    down2p[...] = dot_t(down2_ref[...], order).astype(jnp.bfloat16)

    e_row = lax.broadcasted_iota(jnp.int32, (na, span), 0)
    e_col = lax.broadcasted_iota(jnp.int32, (na, span), 1)
    expand = (e_col // ROWS == e_row).astype(jnp.float32).astype(jnp.bfloat16)
    s_row = lax.broadcasted_iota(jnp.int32, (span, span), 0)
    s_col = lax.broadcasted_iota(jnp.int32, (span, span), 1)

    turn = (s_col == (s_row % ROWS) * na + s_row // ROWS).astype(jnp.float32).astype(jnp.bfloat16)

    @pl.loop(0, parts)
    def _(g):
        by_row = dot(turn, mix2_ref[g]).astype(jnp.bfloat16)
        wide = dot(by_row, expand)
        spread[g] = jnp.where(s_row % ROWS == s_col % ROWS, wide, 0.0).astype(jnp.bfloat16)

    for load in loads[2:]:
        load.wait()

    def run_second(q):
        await_first(q, fwd_recv)
        part = gathered[q].reshape(span, width)
        got = dot(spread[lax.rem(q, parts)], part).astype(jnp.bfloat16)
        second[q] = got.reshape(n_seq, paired, LANES, ROWS, width)

        @pl.loop(0, LANES)
        def _(lane):
            k = q * LANES + lane
            mixed[k, :, me_s] = second[q, me_s, :, lane]
            send_second(q, lane)

    def send_second(q, lane):
        k = q * LANES + lane

        @pl.loop(1, n_seq)
        def _(i):
            other = lax.rem(me_s + i, n_seq)
            pltpu.make_async_remote_copy(
                src_ref=second.at[q, other, :, lane],
                dst_ref=mixed.at[k, :, me_s],
                send_sem=ret_send.at[k],
                recv_sem=ret_recv.at[k],
                device_id={"seq": other},
                device_id_type=MESH,
            ).start()

    def await_second(k, sem):
        others = mixed.at[k, :, pl.ds(0, n_seq - 1)]
        pltpu.make_async_copy(others, others, sem.at[k]).wait()

    def swap(k, src, dst, send_sem, recv_sem):
        @pl.loop(1, n_chan)
        def _(i):
            other = lax.rem(me_c + i, n_chan)
            cols = pl.ds(pl.multiple_of(other * sub, sub), sub)
            pltpu.make_async_remote_copy(
                src_ref=src.at[k, :, cols],
                dst_ref=dst.at[k, :, my_sub],
                send_sem=send_sem.at[k],
                recv_sem=recv_sem.at[k],
                device_id={"chan": other},
                device_id_type=MESH,
            ).start()

        dst[k, :, my_sub] = src[k, :, my_sub]

    def await_swap(k, dst, sem):
        others = dst.at[k, :, pl.ds(0, width - sub)]
        pltpu.make_async_copy(others, others, sem.at[k]).wait()

    run_second(jnp.int32(0))

    @pl.loop(0, units + 2)
    def _(step):
        @pl.when(step < units)
        def _():
            k = step
            q, lane = lax.div(k, LANES), lax.rem(k, LANES)
            s, g = lax.div(q, parts), lax.rem(q, parts)

            @pl.when((lane == 1) & (q + AHEAD < chunks))
            def _():
                send_first(q + AHEAD)

            @pl.when((lane == 1) & (q + 1 < chunks))
            def _():
                run_second(q + 1)

            await_second(k, ret_recv)
            for pair in range(paired):
                x = x_ref[s, pair * LANES + lane, :, g].reshape(half, width).astype(jnp.float32)
                gate = jax.nn.sigmoid(scale_ref[...] * x + bias_ref[...])
                mix = mixed[k, pair].reshape(half, width).astype(jnp.float32)
                hidden[k, pair * half : (pair + 1) * half] = (x + mix * gate).astype(jnp.bfloat16)
            inner1[k] = dot_t(hidden[k], up1_ref[...]).astype(jnp.bfloat16)
            swap(k, inner1, perm1, c1_send, c1_recv)

        @pl.when((step >= 1) & (step < units + 1))
        def _():
            k = step - 1
            await_swap(k, perm1, c1_recv)
            acc[...] = jnp.zeros_like(acc)

            @pl.loop(0, up2_ref.shape[0] // width)
            def _(t):
                tile = pl.ds(pl.multiple_of(t * width, width), width)
                act = jax.nn.gelu(dot_t(perm1[k], up2p[tile, :]), approximate=True)
                acc[...] += dot_t(act.astype(jnp.bfloat16), down1_ref[:, tile])

            inner2[k] = acc[...].astype(jnp.bfloat16)
            swap(k, inner2, perm2, c2_send, c2_recv)

        @pl.when(step >= 2)
        def _():
            k = step - 2
            q, lane = lax.div(k, LANES), lax.rem(k, LANES)
            s, g = lax.div(q, parts), lax.rem(q, parts)
            await_swap(k, perm2, c2_recv)
            got = dot_t(perm2[k], down2p[...])
            got = (hidden[k].astype(jnp.float32) + got).astype(jnp.bfloat16)
            result[k] = got.reshape(paired, n_seq, ROWS, width)
            for pair in range(paired):
                a = pair * LANES + lane
                src, dst = result.at[k, pair], out_ref.at[s, :, g, :, my_cols]

                @pl.when(a == me_c)
                def _(src=src, dst=dst):
                    pltpu.make_async_copy(src, dst, out_local.at[s]).start()

                @pl.when(a != me_c)
                def _(src=src, dst=dst, a=a):
                    pltpu.make_async_remote_copy(
                        src_ref=src,
                        dst_ref=dst,
                        send_sem=out_send.at[s],
                        recv_sem=out_recv.at[s],
                        device_id={"chan": a},
                        device_id_type=MESH,
                    ).start()

    @pl.loop(0, seqs)
    def _(s):
        landed = out_ref.at[s, :, :, :, pl.ds(0, width * (n_chan - 1))]
        pltpu.make_async_copy(landed, landed, out_send.at[s]).wait()
        pltpu.make_async_copy(landed, landed, out_recv.at[s]).wait()
        one = out_ref.at[s, :, :, :, pl.ds(0, width)]
        pltpu.make_async_copy(one, one, out_local.at[s]).wait()

    @pl.loop(0, chunks)
    def _(q):
        await_first(q, fwd_send)

    @pl.loop(0, units)
    def _(k):
        await_second(k, ret_send)
        await_swap(k, perm1, c1_send)
        await_swap(k, perm2, c2_send)


def fused_layer(
    inputs,
    mix_first,
    mix_second,
    gate_scale,
    gate_bias,
    up_first,
    up_second,
    down_first,
    down_second,
):
    n_seq, n_chan = lax.axis_size("seq"), lax.axis_size("chan")
    seqs, rows, width = inputs.shape
    blocks, group = mix_first.shape[0], mix_first.shape[1]
    own_b, na = mix_second.shape[0], mix_second.shape[1]
    parts = own_b // ROWS
    chunks = seqs * parts
    units = chunks * LANES
    paired = blocks // LANES
    bf = jnp.bfloat16
    per_unit = pltpu.VMEM((units, paired * n_seq * ROWS, width), bf)
    by_device = pltpu.VMEM((units, paired, n_seq, ROWS, width), bf)
    dma = pltpu.SemaphoreType.DMA
    out = pl.pallas_call(
        functools.partial(layer_kernel, n_seq, n_chan),
        out_shape=jax.ShapeDtypeStruct((seqs, n_seq, parts, ROWS, width * n_chan), bf),
        in_specs=[pl.BlockSpec(memory_space=pltpu.VMEM)] * 5
        + [pl.BlockSpec(memory_space=pl.ANY)] * 4,
        out_specs=pl.BlockSpec(memory_space=pl.ANY),
        scratch_shapes=[
            pltpu.VMEM((seqs, blocks, n_seq, parts, ROWS, width), bf),
            pltpu.VMEM((chunks, na, ROWS, width), bf),
            pltpu.VMEM((chunks, n_seq, paired, LANES, ROWS, width), bf),
            by_device,
            per_unit,
            per_unit,
            per_unit,
            per_unit,
            per_unit,
            by_device,
            pltpu.VMEM(up_second.shape[1:], bf),
            pltpu.VMEM(down_second.shape[1:], bf),
            pltpu.VMEM((parts, na * ROWS, na * ROWS), bf),
            pltpu.VMEM((paired * n_seq * ROWS, width), jnp.float32),
            pltpu.VMEM(up_first.shape[1:], bf),
            pltpu.VMEM(up_second.shape[1:], bf),
            pltpu.VMEM(down_first.shape[1:], bf),
            pltpu.VMEM(down_second.shape[1:], bf),
            dma((4,)),
            dma((chunks,)),
            dma((chunks,)),
            dma((units,)),
            dma((units,)),
            dma((units,)),
            dma((units,)),
            dma((units,)),
            dma((units,)),
            dma((seqs,)),
            dma((seqs,)),
            dma((seqs,)),
        ],
        compiler_params=pltpu.CompilerParams(
            collective_id=0, has_side_effects=True, vmem_limit_bytes=56 * 1024 * 1024
        ),
    )(
        inputs.reshape(seqs, blocks, n_seq, parts, ROWS, width),
        mix_first,
        mix_second.reshape(parts, ROWS * na, na),
        gate_scale.reshape(1, width),
        gate_bias.reshape(1, width),
        up_first[0],
        up_second[0],
        down_first[0],
        down_second[0],
    )
    return out.reshape(seqs, group, width * n_chan)


def on_device(inputs, mix_first, mix_second, *rest):
    blocks = mix_first.shape[0]
    whole = mix_second.shape[0] % ROWS == 0 and blocks % LANES == 0
    fits = whole and blocks == lax.axis_size("chan")
    run = fused_layer if fits else plain_layer
    return run(inputs, mix_first, mix_second, *rest)


def plain_layer(
    inputs,
    mix_first,
    mix_second,
    gate_scale,
    gate_bias,
    up_first,
    up_second,
    down_first,
    down_second,
):
    seq_count, row_count, chan_width = inputs.shape
    blocks_here = mix_first.shape[0]
    group_width = mix_first.shape[1]
    grouped = inputs.reshape(seq_count, blocks_here, group_width, chan_width)
    first_pass = jnp.einsum(
        "abq,saqc->sabc", mix_first, grouped, preferred_element_type=jnp.float32
    ).astype(jnp.bfloat16)
    mixed_rows = jnp.einsum(
        "bxy,sybc->sxbc",
        mix_second,
        lax.all_to_all(first_pass, "seq", split_axis=2, concat_axis=1, tiled=True),
        preferred_element_type=jnp.float32,
    ).astype(jnp.bfloat16)
    restored = lax.all_to_all(mixed_rows, "seq", split_axis=1, concat_axis=2, tiled=True).reshape(
        seq_count, row_count, chan_width
    )
    residual_in = inputs.astype(jnp.float32)
    hidden = (
        residual_in
        + restored.astype(jnp.float32) * jax.nn.sigmoid(gate_scale * residual_in + gate_bias)
    ).astype(jnp.bfloat16)
    expanded = shard_monarch(hidden, up_first, up_second)
    activated = jax.nn.gelu(expanded, approximate=True).astype(jnp.bfloat16)
    contracted = shard_monarch(activated, down_first, down_second)
    result = (hidden.astype(jnp.float32) + contracted).astype(jnp.bfloat16)
    return lax.all_to_all(result, "chan", split_axis=1, concat_axis=2, tiled=True)


def solution(mesh):
    return jax.shard_map(
        on_device,
        mesh=mesh,
        in_specs=(
            P(None, "seq", "chan"),
            P("seq", None, None),
            P("seq", None, None),
            P("chan"),
            P("chan"),
            P("chan", None, None),
            P("chan", None, None),
            P("chan", None, None),
            P("chan", None, None),
        ),
        out_specs=P(None, ("seq", "chan"), None),
        check_vma=False,
    )
```

```python
import functools

import jax
import jax.numpy as jnp
from jax import lax
from jax.experimental import pallas as pl
from jax.experimental.pallas import tpu as pltpu
from jax.sharding import PartitionSpec as P

MESH = pl.DeviceIdType.MESH
ROWS = 16
LANES = 2
AHEAD = 2
STRIDE = 3


def shard_monarch(values, inner_weight, outer_weight):
    chan_count = lax.axis_size("chan")
    inner_width = inner_weight.shape[1]
    out_width = outer_weight.shape[1]
    sub_width = inner_width // chan_count
    seq_count, row_count = (values.shape[0], values.shape[1])
    inner_rows = jnp.einsum(
        "qp,stp->stq", inner_weight[0], values, preferred_element_type=jnp.float32
    )
    inner_rows = inner_rows.astype(jnp.bfloat16).reshape(
        seq_count, row_count, chan_count, sub_width
    )
    permuted = lax.all_to_all(inner_rows, "chan", split_axis=2, concat_axis=2, tiled=True)
    outer_blocks = outer_weight[0].reshape(out_width, sub_width, chan_count)
    return jnp.einsum("oqc,stcq->sto", outer_blocks, permuted, preferred_element_type=jnp.float32)


def dot(a, b):
    return jnp.dot(a, b, preferred_element_type=jnp.float32)


def dot_t(a, b):
    return lax.dot_general(a, b, (((1,), (1,)), ((), ())), preferred_element_type=jnp.float32)


def layer_kernel(
    n_seq,
    n_chan,
    x_ref,
    mix1_ref,
    mix2_ref,
    scale_ref,
    bias_ref,
    up1_hbm,
    up2_hbm,
    down1_hbm,
    down2_hbm,
    out_ref,
    first,
    gathered,
    second,
    mixed,
    hidden,
    inner1,
    perm1,
    inner2,
    perm2,
    result,
    up2p,
    down2p,
    spread,
    acc,
    up1_ref,
    up2_ref,
    down1_ref,
    down2_ref,
    load_sem,
    fwd_send,
    fwd_recv,
    ret_send,
    ret_recv,
    c1_send,
    c1_recv,
    c2_send,
    c2_recv,
    out_send,
    out_recv,
    out_local,
):
    seqs, blocks, _, parts, _, width = x_ref.shape
    na = n_seq * blocks
    group = n_seq * parts * ROWS
    sub = width // n_chan
    chunks = seqs * parts
    units = chunks * LANES
    paired = blocks // LANES
    half = n_seq * ROWS
    me_s = lax.axis_index("seq")
    me_c = lax.axis_index("chan")

    barrier = pltpu.get_barrier_semaphore()
    for i in range(1, n_seq):
        pl.semaphore_signal(
            barrier, inc=1, device_id={"seq": lax.rem(me_s + i, n_seq)}, device_id_type=MESH
        )
    for i in range(1, n_chan):
        pl.semaphore_signal(
            barrier, inc=1, device_id={"chan": lax.rem(me_c + i, n_chan)}, device_id_type=MESH
        )

    loads = [
        pltpu.make_async_copy(src, dst, load_sem.at[i])
        for i, (src, dst) in enumerate(
            [(up2_hbm, up2_ref), (down2_hbm, down2_ref), (up1_hbm, up1_ref), (down1_hbm, down1_ref)]
        )
    ]
    for load in loads:
        load.start()

    my_a = pl.ds(me_s * blocks, blocks)
    my_sub = pl.ds(pl.multiple_of(me_c * sub, sub), sub)
    my_cols = pl.ds(pl.multiple_of(me_c * width, width), width)

    def run_first(s):
        @pl.loop(0, blocks)
        def _(a):
            got = dot(mix1_ref[a], x_ref[s, a].reshape(group, width)).astype(jnp.bfloat16)
            first[s, a] = got.reshape(n_seq, parts, ROWS, width)

        for g in range(parts):
            gathered[s * parts + g, my_a] = first[s, :, me_s, g]

    def send_first(q):
        @pl.loop(1, n_seq)
        def _(i):
            other = lax.rem(me_s + STRIDE * i, n_seq)
            pltpu.make_async_remote_copy(
                src_ref=first.at[lax.div(q, parts), :, other, lax.rem(q, parts)],
                dst_ref=gathered.at[q, my_a],
                send_sem=fwd_send.at[q],
                recv_sem=fwd_recv.at[q],
                device_id={"seq": other},
                device_id_type=MESH,
            ).start()

    def await_first(q, sem):
        others = gathered.at[q, pl.ds(0, na - blocks)]
        pltpu.make_async_copy(others, others, sem.at[q]).wait()

    run_first(0)
    pl.semaphore_wait(barrier, n_seq + n_chan - 2)
    for q in range(min(AHEAD, parts)):
        send_first(jnp.int32(q))

    @pl.loop(1, seqs)
    def _(s):
        run_first(s)

    for load in loads[:2]:
        load.wait()

    span = na * ROWS
    row = lax.broadcasted_iota(jnp.int32, (width, width), 0)
    col = lax.broadcasted_iota(jnp.int32, (width, width), 1)
    order = (col == (row % sub) * n_chan + row // sub).astype(jnp.float32).astype(jnp.bfloat16)

    @pl.loop(0, up2_ref.shape[0] // width)
    def _(t):
        rows = pl.ds(pl.multiple_of(t * width, width), width)
        up2p[rows, :] = dot_t(up2_ref[rows, :], order).astype(jnp.bfloat16)

    down2p[...] = dot_t(down2_ref[...], order).astype(jnp.bfloat16)

    e_row = lax.broadcasted_iota(jnp.int32, (na, span), 0)
    e_col = lax.broadcasted_iota(jnp.int32, (na, span), 1)
    expand = (e_col // ROWS == e_row).astype(jnp.float32).astype(jnp.bfloat16)
    s_row = lax.broadcasted_iota(jnp.int32, (span, span), 0)
    s_col = lax.broadcasted_iota(jnp.int32, (span, span), 1)

    turn = (s_col == (s_row % ROWS) * na + s_row // ROWS).astype(jnp.float32).astype(jnp.bfloat16)

    @pl.loop(0, parts)
    def _(g):
        by_row = dot(turn, mix2_ref[g]).astype(jnp.bfloat16)
        wide = dot(by_row, expand)
        spread[g] = jnp.where(s_row % ROWS == s_col % ROWS, wide, 0.0).astype(jnp.bfloat16)

    for load in loads[2:]:
        load.wait()

    def run_second(q):
        await_first(q, fwd_recv)
        part = gathered[q].reshape(span, width)
        got = dot(spread[lax.rem(q, parts)], part).astype(jnp.bfloat16)
        second[q] = got.reshape(n_seq, paired, LANES, ROWS, width)

        @pl.loop(0, LANES)
        def _(lane):
            k = q * LANES + lane
            mixed[k, :, me_s] = second[q, me_s, :, lane]
            send_second(q, lane)

    def send_second(q, lane):
        k = q * LANES + lane

        @pl.loop(1, n_seq)
        def _(i):
            other = lax.rem(me_s + STRIDE * i, n_seq)
            pltpu.make_async_remote_copy(
                src_ref=second.at[q, other, :, lane],
                dst_ref=mixed.at[k, :, me_s],
                send_sem=ret_send.at[k],
                recv_sem=ret_recv.at[k],
                device_id={"seq": other},
                device_id_type=MESH,
            ).start()

    def await_second(k, sem):
        others = mixed.at[k, :, pl.ds(0, n_seq - 1)]
        pltpu.make_async_copy(others, others, sem.at[k]).wait()

    def swap(k, src, dst, send_sem, recv_sem):
        @pl.loop(1, n_chan)
        def _(i):
            other = lax.rem(me_c + i, n_chan)
            cols = pl.ds(pl.multiple_of(other * sub, sub), sub)
            pltpu.make_async_remote_copy(
                src_ref=src.at[k, :, cols],
                dst_ref=dst.at[k, :, my_sub],
                send_sem=send_sem.at[k],
                recv_sem=recv_sem.at[k],
                device_id={"chan": other},
                device_id_type=MESH,
            ).start()

        dst[k, :, my_sub] = src[k, :, my_sub]

    def await_swap(k, dst, sem):
        others = dst.at[k, :, pl.ds(0, width - sub)]
        pltpu.make_async_copy(others, others, sem.at[k]).wait()

    run_second(jnp.int32(0))

    @pl.loop(0, units + 2)
    def _(step):
        @pl.when(step < units)
        def _():
            k = step
            q, lane = lax.div(k, LANES), lax.rem(k, LANES)
            s, g = lax.div(q, parts), lax.rem(q, parts)

            @pl.when((lane == 1) & (q + AHEAD < chunks))
            def _():
                send_first(q + AHEAD)

            @pl.when((lane == 1) & (q + 1 < chunks))
            def _():
                run_second(q + 1)

            await_second(k, ret_recv)
            for pair in range(paired):
                x = x_ref[s, pair * LANES + lane, :, g].reshape(half, width).astype(jnp.float32)
                gate = jax.nn.sigmoid(scale_ref[...] * x + bias_ref[...])
                mix = mixed[k, pair].reshape(half, width).astype(jnp.float32)
                hidden[k, pair * half : (pair + 1) * half] = (x + mix * gate).astype(jnp.bfloat16)
            inner1[k] = dot_t(hidden[k], up1_ref[...]).astype(jnp.bfloat16)
            swap(k, inner1, perm1, c1_send, c1_recv)

        @pl.when((step >= 1) & (step < units + 1))
        def _():
            k = step - 1
            await_swap(k, perm1, c1_recv)
            acc[...] = jnp.zeros_like(acc)

            @pl.loop(0, up2_ref.shape[0] // width)
            def _(t):
                tile = pl.ds(pl.multiple_of(t * width, width), width)
                act = jax.nn.gelu(dot_t(perm1[k], up2p[tile, :]), approximate=True)
                acc[...] += dot_t(act.astype(jnp.bfloat16), down1_ref[:, tile])

            inner2[k] = acc[...].astype(jnp.bfloat16)
            swap(k, inner2, perm2, c2_send, c2_recv)

        @pl.when(step >= 2)
        def _():
            k = step - 2
            q, lane = lax.div(k, LANES), lax.rem(k, LANES)
            s, g = lax.div(q, parts), lax.rem(q, parts)
            await_swap(k, perm2, c2_recv)
            got = dot_t(perm2[k], down2p[...])
            got = (hidden[k].astype(jnp.float32) + got).astype(jnp.bfloat16)
            result[k] = got.reshape(paired, n_seq, ROWS, width)
            for pair in range(paired):
                a = pair * LANES + lane
                src, dst = result.at[k, pair], out_ref.at[s, :, g, :, my_cols]

                @pl.when(a == me_c)
                def _(src=src, dst=dst):
                    pltpu.make_async_copy(src, dst, out_local.at[s]).start()

                @pl.when(a != me_c)
                def _(src=src, dst=dst, a=a):
                    pltpu.make_async_remote_copy(
                        src_ref=src,
                        dst_ref=dst,
                        send_sem=out_send.at[s],
                        recv_sem=out_recv.at[s],
                        device_id={"chan": a},
                        device_id_type=MESH,
                    ).start()

    @pl.loop(0, seqs)
    def _(s):
        landed = out_ref.at[s, :, :, :, pl.ds(0, width * (n_chan - 1))]
        pltpu.make_async_copy(landed, landed, out_send.at[s]).wait()
        pltpu.make_async_copy(landed, landed, out_recv.at[s]).wait()
        one = out_ref.at[s, :, :, :, pl.ds(0, width)]
        pltpu.make_async_copy(one, one, out_local.at[s]).wait()

    @pl.loop(0, chunks)
    def _(q):
        await_first(q, fwd_send)

    @pl.loop(0, units)
    def _(k):
        await_second(k, ret_send)
        await_swap(k, perm1, c1_send)
        await_swap(k, perm2, c2_send)


def fused_layer(
    inputs,
    mix_first,
    mix_second,
    gate_scale,
    gate_bias,
    up_first,
    up_second,
    down_first,
    down_second,
):
    n_seq, n_chan = lax.axis_size("seq"), lax.axis_size("chan")
    seqs, rows, width = inputs.shape
    blocks, group = mix_first.shape[0], mix_first.shape[1]
    own_b, na = mix_second.shape[0], mix_second.shape[1]
    parts = own_b // ROWS
    chunks = seqs * parts
    units = chunks * LANES
    paired = blocks // LANES
    bf = jnp.bfloat16
    per_unit = pltpu.VMEM((units, paired * n_seq * ROWS, width), bf)
    by_device = pltpu.VMEM((units, paired, n_seq, ROWS, width), bf)
    dma = pltpu.SemaphoreType.DMA
    out = pl.pallas_call(
        functools.partial(layer_kernel, n_seq, n_chan),
        out_shape=jax.ShapeDtypeStruct((seqs, n_seq, parts, ROWS, width * n_chan), bf),
        in_specs=[pl.BlockSpec(memory_space=pltpu.VMEM)] * 5
        + [pl.BlockSpec(memory_space=pl.ANY)] * 4,
        out_specs=pl.BlockSpec(memory_space=pl.ANY),
        scratch_shapes=[
            pltpu.VMEM((seqs, blocks, n_seq, parts, ROWS, width), bf),
            pltpu.VMEM((chunks, na, ROWS, width), bf),
            pltpu.VMEM((chunks, n_seq, paired, LANES, ROWS, width), bf),
            by_device,
            per_unit,
            per_unit,
            per_unit,
            per_unit,
            per_unit,
            by_device,
            pltpu.VMEM(up_second.shape[1:], bf),
            pltpu.VMEM(down_second.shape[1:], bf),
            pltpu.VMEM((parts, na * ROWS, na * ROWS), bf),
            pltpu.VMEM((paired * n_seq * ROWS, width), jnp.float32),
            pltpu.VMEM(up_first.shape[1:], bf),
            pltpu.VMEM(up_second.shape[1:], bf),
            pltpu.VMEM(down_first.shape[1:], bf),
            pltpu.VMEM(down_second.shape[1:], bf),
            dma((4,)),
            dma((chunks,)),
            dma((chunks,)),
            dma((units,)),
            dma((units,)),
            dma((units,)),
            dma((units,)),
            dma((units,)),
            dma((units,)),
            dma((seqs,)),
            dma((seqs,)),
            dma((seqs,)),
        ],
        compiler_params=pltpu.CompilerParams(
            collective_id=0, has_side_effects=True, vmem_limit_bytes=56 * 1024 * 1024
        ),
    )(
        inputs.reshape(seqs, blocks, n_seq, parts, ROWS, width),
        mix_first,
        mix_second.reshape(parts, ROWS * na, na),
        gate_scale.reshape(1, width),
        gate_bias.reshape(1, width),
        up_first[0],
        up_second[0],
        down_first[0],
        down_second[0],
    )
    return out.reshape(seqs, group, width * n_chan)


def on_device(inputs, mix_first, mix_second, *rest):
    blocks = mix_first.shape[0]
    whole = mix_second.shape[0] % ROWS == 0 and blocks % LANES == 0
    fits = whole and blocks == lax.axis_size("chan") and lax.axis_size("seq") % STRIDE != 0
    run = fused_layer if fits else plain_layer
    return run(inputs, mix_first, mix_second, *rest)


def plain_layer(
    inputs,
    mix_first,
    mix_second,
    gate_scale,
    gate_bias,
    up_first,
    up_second,
    down_first,
    down_second,
):
    seq_count, row_count, chan_width = inputs.shape
    blocks_here = mix_first.shape[0]
    group_width = mix_first.shape[1]
    grouped = inputs.reshape(seq_count, blocks_here, group_width, chan_width)
    first_pass = jnp.einsum(
        "abq,saqc->sabc", mix_first, grouped, preferred_element_type=jnp.float32
    ).astype(jnp.bfloat16)
    mixed_rows = jnp.einsum(
        "bxy,sybc->sxbc",
        mix_second,
        lax.all_to_all(first_pass, "seq", split_axis=2, concat_axis=1, tiled=True),
        preferred_element_type=jnp.float32,
    ).astype(jnp.bfloat16)
    restored = lax.all_to_all(mixed_rows, "seq", split_axis=1, concat_axis=2, tiled=True).reshape(
        seq_count, row_count, chan_width
    )
    residual_in = inputs.astype(jnp.float32)
    hidden = (
        residual_in
        + restored.astype(jnp.float32) * jax.nn.sigmoid(gate_scale * residual_in + gate_bias)
    ).astype(jnp.bfloat16)
    expanded = shard_monarch(hidden, up_first, up_second)
    activated = jax.nn.gelu(expanded, approximate=True).astype(jnp.bfloat16)
    contracted = shard_monarch(activated, down_first, down_second)
    result = (hidden.astype(jnp.float32) + contracted).astype(jnp.bfloat16)
    return lax.all_to_all(result, "chan", split_axis=1, concat_axis=2, tiled=True)


def solution(mesh):
    return jax.shard_map(
        on_device,
        mesh=mesh,
        in_specs=(
            P(None, "seq", "chan"),
            P("seq", None, None),
            P("seq", None, None),
            P("chan"),
            P("chan"),
            P("chan", None, None),
            P("chan", None, None),
            P("chan", None, None),
            P("chan", None, None),
        ),
        out_specs=P(None, ("seq", "chan"), None),
        check_vma=False,
    )
```

```python
import functools

import jax
import jax.numpy as jnp
from jax import lax
from jax.experimental import pallas as pl
from jax.experimental.pallas import tpu as pltpu
from jax.sharding import PartitionSpec as P

MESH = pl.DeviceIdType.MESH
ROWS = 16
LANES = 2
AHEAD = 2
STEPS = ((3, 6, 1, 4, 7, 2, 5), (2, 5, 4, 1, 3, 6, 7))
PIECES = 4


def shard_monarch(values, inner_weight, outer_weight):
    chan_count = lax.axis_size("chan")
    inner_width = inner_weight.shape[1]
    out_width = outer_weight.shape[1]
    sub_width = inner_width // chan_count
    seq_count, row_count = (values.shape[0], values.shape[1])
    inner_rows = jnp.einsum(
        "qp,stp->stq", inner_weight[0], values, preferred_element_type=jnp.float32
    )
    inner_rows = inner_rows.astype(jnp.bfloat16).reshape(
        seq_count, row_count, chan_count, sub_width
    )
    permuted = lax.all_to_all(inner_rows, "chan", split_axis=2, concat_axis=2, tiled=True)
    outer_blocks = outer_weight[0].reshape(out_width, sub_width, chan_count)
    return jnp.einsum("oqc,stcq->sto", outer_blocks, permuted, preferred_element_type=jnp.float32)


def dot(a, b):
    return jnp.dot(a, b, preferred_element_type=jnp.float32)


def dot_t(a, b):
    return lax.dot_general(a, b, (((1,), (1,)), ((), ())), preferred_element_type=jnp.float32)


def layer_kernel(
    n_seq,
    n_chan,
    x_ref,
    mix1_ref,
    mix2_ref,
    scale_ref,
    bias_ref,
    up1_hbm,
    up2_hbm,
    down1_hbm,
    down2_hbm,
    out_ref,
    first,
    gathered,
    second,
    mixed,
    hidden,
    inner1,
    perm1,
    inner2,
    perm2,
    result,
    up2p,
    down2p,
    spread,
    acc,
    up1_ref,
    up2_ref,
    down1_ref,
    down2_ref,
    load_sem,
    fwd_send,
    fwd_recv,
    ret_send,
    ret_recv,
    c1_send,
    c1_recv,
    c2_send,
    c2_recv,
    out_send,
    out_recv,
    out_local,
):
    seqs, blocks, _, parts, _, width = x_ref.shape
    na = n_seq * blocks
    group = n_seq * parts * ROWS
    sub = width // n_chan
    chunks = seqs * parts
    units = chunks * LANES
    paired = blocks // LANES
    half = n_seq * ROWS
    me_s = lax.axis_index("seq")
    me_c = lax.axis_index("chan")
    core = lax.rem(me_c, 2)

    barrier = pltpu.get_barrier_semaphore()
    for i in range(1, n_seq):
        pl.semaphore_signal(
            barrier, inc=1, device_id={"seq": lax.rem(me_s + i, n_seq)}, device_id_type=MESH
        )
    for i in range(1, n_chan):
        pl.semaphore_signal(
            barrier, inc=1, device_id={"chan": lax.rem(me_c + i, n_chan)}, device_id_type=MESH
        )

    loads = [
        pltpu.make_async_copy(src, dst, load_sem.at[i])
        for i, (src, dst) in enumerate(
            [(up2_hbm, up2_ref), (down2_hbm, down2_ref), (up1_hbm, up1_ref), (down1_hbm, down1_ref)]
        )
    ]
    for load in loads:
        load.start()

    my_a = pl.ds(me_s * blocks, blocks)
    my_sub = pl.ds(pl.multiple_of(me_c * sub, sub), sub)
    my_cols = pl.ds(pl.multiple_of(me_c * width, width), width)

    def run_first(s):
        @pl.loop(0, blocks)
        def _(a):
            got = dot(mix1_ref[a], x_ref[s, a].reshape(group, width)).astype(jnp.bfloat16)
            first[s, a] = got.reshape(n_seq, parts, ROWS, width)

        for g in range(parts):
            gathered[s * parts + g, my_a] = first[s, :, me_s, g]

    def send_first(q):
        for even, odd in zip(*STEPS):
            other = lax.rem(me_s + even + core * (odd - even), n_seq)
            pltpu.make_async_remote_copy(
                src_ref=first.at[lax.div(q, parts), :, other, lax.rem(q, parts)],
                dst_ref=gathered.at[q, my_a],
                send_sem=fwd_send.at[q],
                recv_sem=fwd_recv.at[q],
                device_id={"seq": other},
                device_id_type=MESH,
            ).start()

    def await_first(q, sem):
        others = gathered.at[q, pl.ds(0, na - blocks)]
        pltpu.make_async_copy(others, others, sem.at[q]).wait()

    run_first(0)
    pl.semaphore_wait(barrier, n_seq + n_chan - 2)
    for q in range(min(AHEAD, parts)):
        send_first(jnp.int32(q))

    @pl.loop(1, seqs)
    def _(s):
        run_first(s)

    for load in loads[:2]:
        load.wait()

    span = na * ROWS
    row = lax.broadcasted_iota(jnp.int32, (width, width), 0)
    col = lax.broadcasted_iota(jnp.int32, (width, width), 1)
    order = (col == (row % sub) * n_chan + row // sub).astype(jnp.float32).astype(jnp.bfloat16)

    @pl.loop(0, up2_ref.shape[0] // width)
    def _(t):
        rows = pl.ds(pl.multiple_of(t * width, width), width)
        up2p[rows, :] = dot_t(up2_ref[rows, :], order).astype(jnp.bfloat16)

    down2p[...] = dot_t(down2_ref[...], order).astype(jnp.bfloat16)

    e_row = lax.broadcasted_iota(jnp.int32, (na, span), 0)
    e_col = lax.broadcasted_iota(jnp.int32, (na, span), 1)
    expand = (e_col // ROWS == e_row).astype(jnp.float32).astype(jnp.bfloat16)
    s_row = lax.broadcasted_iota(jnp.int32, (span, span), 0)
    s_col = lax.broadcasted_iota(jnp.int32, (span, span), 1)

    turn = (s_col == (s_row % ROWS) * na + s_row // ROWS).astype(jnp.float32).astype(jnp.bfloat16)

    @pl.loop(0, parts)
    def _(g):
        by_row = dot(turn, mix2_ref[g]).astype(jnp.bfloat16)
        wide = dot(by_row, expand)
        spread[g] = jnp.where(s_row % ROWS == s_col % ROWS, wide, 0.0).astype(jnp.bfloat16)

    for load in loads[2:]:
        load.wait()

    def run_second(q):
        await_first(q, fwd_recv)
        part = gathered[q].reshape(span, width)
        got = dot(spread[lax.rem(q, parts)], part).astype(jnp.bfloat16)
        second[q] = got.reshape(n_seq, paired, LANES, ROWS, width)

        @pl.loop(0, LANES)
        def _(lane):
            k = q * LANES + lane
            mixed[k, :, me_s] = second[q, me_s, :, lane]
            send_second(q, lane)

    def send_second(q, lane):
        k = q * LANES + lane

        for even, odd in zip(*STEPS):
            other = lax.rem(me_s + even + core * (odd - even), n_seq)
            pltpu.make_async_remote_copy(
                src_ref=second.at[q, other, :, lane],
                dst_ref=mixed.at[k, :, me_s],
                send_sem=ret_send.at[k],
                recv_sem=ret_recv.at[k],
                device_id={"seq": other},
                device_id_type=MESH,
            ).start()

    def await_second(k, sem):
        others = mixed.at[k, :, pl.ds(0, n_seq - 1)]
        pltpu.make_async_copy(others, others, sem.at[k]).wait()

    def swap(k, src, dst, send_sem, recv_sem):
        @pl.loop(1, n_chan)
        def _(i):
            other = lax.rem(me_c + i, n_chan)
            cols = pl.ds(pl.multiple_of(other * sub, sub), sub)
            pltpu.make_async_remote_copy(
                src_ref=src.at[k, :, cols],
                dst_ref=dst.at[k, :, my_sub],
                send_sem=send_sem.at[k],
                recv_sem=recv_sem.at[k],
                device_id={"chan": other},
                device_id_type=MESH,
            ).start()

        dst[k, :, my_sub] = src[k, :, my_sub]

    def await_swap(k, dst, sem):
        others = dst.at[k, :, pl.ds(0, width - sub)]
        pltpu.make_async_copy(others, others, sem.at[k]).wait()

    run_second(jnp.int32(0))

    @pl.loop(0, units + 2)
    def _(step):
        @pl.when(step < units)
        def _():
            k = step
            q, lane = lax.div(k, LANES), lax.rem(k, LANES)
            s, g = lax.div(q, parts), lax.rem(q, parts)

            @pl.when((lane == 1) & (q + AHEAD < chunks))
            def _():
                send_first(q + AHEAD)

            @pl.when((lane == 1) & (q + 1 < chunks))
            def _():
                run_second(q + 1)

            await_second(k, ret_recv)
            for pair in range(paired):
                x = x_ref[s, pair * LANES + lane, :, g].reshape(half, width).astype(jnp.float32)
                gate = jax.nn.sigmoid(scale_ref[...] * x + bias_ref[...])
                mix = mixed[k, pair].reshape(half, width).astype(jnp.float32)
                hidden[k, pair * half : (pair + 1) * half] = (x + mix * gate).astype(jnp.bfloat16)
            inner1[k] = dot_t(hidden[k], up1_ref[...]).astype(jnp.bfloat16)
            swap(k, inner1, perm1, c1_send, c1_recv)

        @pl.when((step >= 1) & (step < units + 1))
        def _():
            k = step - 1
            await_swap(k, perm1, c1_recv)
            acc[...] = jnp.zeros_like(acc)

            @pl.loop(0, up2_ref.shape[0] // width)
            def _(t):
                tile = pl.ds(pl.multiple_of(t * width, width), width)
                act = jax.nn.gelu(dot_t(perm1[k], up2p[tile, :]), approximate=True)
                acc[...] += dot_t(act.astype(jnp.bfloat16), down1_ref[:, tile])

            inner2[k] = acc[...].astype(jnp.bfloat16)
            swap(k, inner2, perm2, c2_send, c2_recv)

        @pl.when(step >= 2)
        def _():
            k = step - 2
            q, lane = lax.div(k, LANES), lax.rem(k, LANES)
            s, g = lax.div(q, parts), lax.rem(q, parts)
            await_swap(k, perm2, c2_recv)
            got = dot_t(perm2[k], down2p[...])
            got = (hidden[k].astype(jnp.float32) + got).astype(jnp.bfloat16)
            result[k] = got.reshape(paired, n_seq, ROWS, width)
            for pair in range(paired):
                a = pair * LANES + lane
                src, dst = result.at[k, pair], out_ref.at[s, :, g, :, my_cols]

                @pl.when(a == me_c)
                def _(src=src, dst=dst):
                    pltpu.make_async_copy(src, dst, out_local.at[s]).start()

                @pl.when(a != me_c)
                def _(src=src, dst=dst, a=a):
                    pltpu.make_async_remote_copy(
                        src_ref=src,
                        dst_ref=dst,
                        send_sem=out_send.at[s],
                        recv_sem=out_recv.at[s],
                        device_id={"chan": a},
                        device_id_type=MESH,
                    ).start()

    @pl.loop(0, seqs)
    def _(s):
        landed = out_ref.at[s, :, :, :, pl.ds(0, width * (n_chan - 1))]
        pltpu.make_async_copy(landed, landed, out_send.at[s]).wait()
        pltpu.make_async_copy(landed, landed, out_recv.at[s]).wait()
        one = out_ref.at[s, :, :, :, pl.ds(0, width)]
        pltpu.make_async_copy(one, one, out_local.at[s]).wait()

    @pl.loop(0, chunks)
    def _(q):
        await_first(q, fwd_send)

    @pl.loop(0, units)
    def _(k):
        await_second(k, ret_send)
        await_swap(k, perm1, c1_send)
        await_swap(k, perm2, c2_send)


def copy_kernel(src_ref, dst_ref, sem):
    seqs, rows = src_ref.shape[0], src_ref.shape[1] // PIECES
    copies = [
        pltpu.make_async_copy(
            src_ref.at[s, pl.ds(i * rows, rows)],
            dst_ref.at[s, pl.ds(i * rows, rows)],
            sem.at[s * PIECES + i],
        )
        for s in range(seqs)
        for i in range(PIECES)
    ]
    for copy in copies:
        copy.start()
    for copy in copies:
        copy.wait()


def hand_over(array):
    return pl.pallas_call(
        copy_kernel,
        out_shape=jax.ShapeDtypeStruct(array.shape, array.dtype),
        in_specs=[pl.BlockSpec(memory_space=pl.ANY)],
        out_specs=pl.BlockSpec(memory_space=pl.ANY),
        scratch_shapes=[pltpu.SemaphoreType.DMA((array.shape[0] * PIECES,))],
    )(array)


def fused_layer(
    inputs,
    mix_first,
    mix_second,
    gate_scale,
    gate_bias,
    up_first,
    up_second,
    down_first,
    down_second,
):
    n_seq, n_chan = lax.axis_size("seq"), lax.axis_size("chan")
    seqs, rows, width = inputs.shape
    blocks, group = mix_first.shape[0], mix_first.shape[1]
    own_b, na = mix_second.shape[0], mix_second.shape[1]
    parts = own_b // ROWS
    chunks = seqs * parts
    units = chunks * LANES
    paired = blocks // LANES
    bf = jnp.bfloat16
    per_unit = pltpu.VMEM((units, paired * n_seq * ROWS, width), bf)
    by_device = pltpu.VMEM((units, paired, n_seq, ROWS, width), bf)
    dma = pltpu.SemaphoreType.DMA
    out = pl.pallas_call(
        functools.partial(layer_kernel, n_seq, n_chan),
        out_shape=jax.ShapeDtypeStruct((seqs, n_seq, parts, ROWS, width * n_chan), bf),
        in_specs=[pl.BlockSpec(memory_space=pltpu.VMEM)] * 5
        + [pl.BlockSpec(memory_space=pl.ANY)] * 4,
        out_specs=pl.BlockSpec(memory_space=pl.ANY),
        scratch_shapes=[
            pltpu.VMEM((seqs, blocks, n_seq, parts, ROWS, width), bf),
            pltpu.VMEM((chunks, na, ROWS, width), bf),
            pltpu.VMEM((chunks, n_seq, paired, LANES, ROWS, width), bf),
            by_device,
            per_unit,
            per_unit,
            per_unit,
            per_unit,
            per_unit,
            by_device,
            pltpu.VMEM(up_second.shape[1:], bf),
            pltpu.VMEM(down_second.shape[1:], bf),
            pltpu.VMEM((parts, na * ROWS, na * ROWS), bf),
            pltpu.VMEM((paired * n_seq * ROWS, width), jnp.float32),
            pltpu.VMEM(up_first.shape[1:], bf),
            pltpu.VMEM(up_second.shape[1:], bf),
            pltpu.VMEM(down_first.shape[1:], bf),
            pltpu.VMEM(down_second.shape[1:], bf),
            dma((4,)),
            dma((chunks,)),
            dma((chunks,)),
            dma((units,)),
            dma((units,)),
            dma((units,)),
            dma((units,)),
            dma((units,)),
            dma((units,)),
            dma((seqs,)),
            dma((seqs,)),
            dma((seqs,)),
        ],
        compiler_params=pltpu.CompilerParams(
            collective_id=0, has_side_effects=True, vmem_limit_bytes=56 * 1024 * 1024
        ),
    )(
        inputs.reshape(seqs, blocks, n_seq, parts, ROWS, width),
        mix_first,
        mix_second.reshape(parts, ROWS * na, na),
        gate_scale.reshape(1, width),
        gate_bias.reshape(1, width),
        up_first[0],
        up_second[0],
        down_first[0],
        down_second[0],
    )
    return hand_over(out.reshape(seqs, group, width * n_chan))


def on_device(inputs, mix_first, mix_second, *rest):
    blocks = mix_first.shape[0]
    whole = mix_second.shape[0] % ROWS == 0 and blocks % LANES == 0
    fits = whole and blocks == lax.axis_size("chan") and lax.axis_size("seq") == len(STEPS[0]) + 1
    run = fused_layer if fits else plain_layer
    return run(inputs, mix_first, mix_second, *rest)


def plain_layer(
    inputs,
    mix_first,
    mix_second,
    gate_scale,
    gate_bias,
    up_first,
    up_second,
    down_first,
    down_second,
):
    seq_count, row_count, chan_width = inputs.shape
    blocks_here = mix_first.shape[0]
    group_width = mix_first.shape[1]
    grouped = inputs.reshape(seq_count, blocks_here, group_width, chan_width)
    first_pass = jnp.einsum(
        "abq,saqc->sabc", mix_first, grouped, preferred_element_type=jnp.float32
    ).astype(jnp.bfloat16)
    mixed_rows = jnp.einsum(
        "bxy,sybc->sxbc",
        mix_second,
        lax.all_to_all(first_pass, "seq", split_axis=2, concat_axis=1, tiled=True),
        preferred_element_type=jnp.float32,
    ).astype(jnp.bfloat16)
    restored = lax.all_to_all(mixed_rows, "seq", split_axis=1, concat_axis=2, tiled=True).reshape(
        seq_count, row_count, chan_width
    )
    residual_in = inputs.astype(jnp.float32)
    hidden = (
        residual_in
        + restored.astype(jnp.float32) * jax.nn.sigmoid(gate_scale * residual_in + gate_bias)
    ).astype(jnp.bfloat16)
    expanded = shard_monarch(hidden, up_first, up_second)
    activated = jax.nn.gelu(expanded, approximate=True).astype(jnp.bfloat16)
    contracted = shard_monarch(activated, down_first, down_second)
    result = (hidden.astype(jnp.float32) + contracted).astype(jnp.bfloat16)
    return lax.all_to_all(result, "chan", split_axis=1, concat_axis=2, tiled=True)


def solution(mesh):
    return jax.shard_map(
        on_device,
        mesh=mesh,
        in_specs=(
            P(None, "seq", "chan"),
            P("seq", None, None),
            P("seq", None, None),
            P("chan"),
            P("chan"),
            P("chan", None, None),
            P("chan", None, None),
            P("chan", None, None),
            P("chan", None, None),
        ),
        out_specs=P(None, ("seq", "chan"), None),
        check_vma=False,
    )
```

```python
import functools

import jax
import jax.numpy as jnp
from jax import lax
from jax.experimental import pallas as pl
from jax.experimental.pallas import tpu as pltpu
from jax.sharding import PartitionSpec as P

MESH = pl.DeviceIdType.MESH
ROWS = 16
LANES = 2
AHEAD = 2
STRIDE = 3


def shard_monarch(values, inner_weight, outer_weight):
    chan_count = lax.axis_size("chan")
    inner_width = inner_weight.shape[1]
    out_width = outer_weight.shape[1]
    sub_width = inner_width // chan_count
    seq_count, row_count = (values.shape[0], values.shape[1])
    inner_rows = jnp.einsum(
        "qp,stp->stq", inner_weight[0], values, preferred_element_type=jnp.float32
    )
    inner_rows = inner_rows.astype(jnp.bfloat16).reshape(
        seq_count, row_count, chan_count, sub_width
    )
    permuted = lax.all_to_all(inner_rows, "chan", split_axis=2, concat_axis=2, tiled=True)
    outer_blocks = outer_weight[0].reshape(out_width, sub_width, chan_count)
    return jnp.einsum("oqc,stcq->sto", outer_blocks, permuted, preferred_element_type=jnp.float32)


def dot(a, b):
    return jnp.dot(a, b, preferred_element_type=jnp.float32)


def dot_t(a, b):
    return lax.dot_general(a, b, (((1,), (1,)), ((), ())), preferred_element_type=jnp.float32)


def layer_kernel(
    n_seq,
    n_chan,
    x_ref,
    mix1_ref,
    mix2_ref,
    scale_ref,
    bias_ref,
    up1_hbm,
    up2_hbm,
    down1_hbm,
    down2_hbm,
    out_ref,
    first,
    gathered,
    second,
    mixed,
    hidden,
    inner1,
    perm1,
    inner2,
    perm2,
    result,
    up2p,
    down2p,
    spread,
    acc,
    up1_ref,
    up2_ref,
    down1_ref,
    down2_ref,
    load_sem,
    fwd_send,
    fwd_recv,
    ret_send,
    ret_recv,
    c1_send,
    c1_recv,
    c2_send,
    c2_recv,
    out_send,
    out_recv,
    out_local,
):
    seqs, blocks, _, parts, _, width = x_ref.shape
    na = n_seq * blocks
    group = n_seq * parts * ROWS
    sub = width // n_chan
    chunks = seqs * parts
    units = chunks * LANES
    paired = blocks // LANES
    half = n_seq * ROWS
    me_s = lax.axis_index("seq")
    me_c = lax.axis_index("chan")

    barrier = pltpu.get_barrier_semaphore()
    for i in range(1, n_seq):
        pl.semaphore_signal(
            barrier, inc=1, device_id={"seq": lax.rem(me_s + i, n_seq)}, device_id_type=MESH
        )
    for i in range(1, n_chan):
        pl.semaphore_signal(
            barrier, inc=1, device_id={"chan": lax.rem(me_c + i, n_chan)}, device_id_type=MESH
        )

    loads = [
        pltpu.make_async_copy(src, dst, load_sem.at[i])
        for i, (src, dst) in enumerate(
            [(up2_hbm, up2_ref), (down2_hbm, down2_ref), (up1_hbm, up1_ref), (down1_hbm, down1_ref)]
        )
    ]
    for load in loads:
        load.start()

    my_a = pl.ds(me_s * blocks, blocks)
    my_sub = pl.ds(pl.multiple_of(me_c * sub, sub), sub)
    my_cols = pl.ds(pl.multiple_of(me_c * width, width), width)

    def run_first(s):
        @pl.loop(0, blocks)
        def _(a):
            got = dot(mix1_ref[a], x_ref[s, a].reshape(group, width)).astype(jnp.bfloat16)
            first[s, a] = got.reshape(n_seq, parts, ROWS, width)

        for g in range(parts):
            gathered[s * parts + g, my_a] = first[s, :, me_s, g]

    def send_first(q):
        @pl.loop(1, n_seq)
        def _(i):
            other = lax.rem(me_s + STRIDE * i, n_seq)
            pltpu.make_async_remote_copy(
                src_ref=first.at[lax.div(q, parts), :, other, lax.rem(q, parts)],
                dst_ref=gathered.at[q, my_a],
                send_sem=fwd_send.at[q],
                recv_sem=fwd_recv.at[q],
                device_id={"seq": other},
                device_id_type=MESH,
            ).start()

    def await_first(q, sem):
        others = gathered.at[q, pl.ds(0, na - blocks)]
        pltpu.make_async_copy(others, others, sem.at[q]).wait()

    run_first(0)
    pl.semaphore_wait(barrier, n_seq + n_chan - 2)
    for q in range(min(AHEAD, parts)):
        send_first(jnp.int32(q))

    @pl.loop(1, seqs)
    def _(s):
        run_first(s)

    for load in loads[:2]:
        load.wait()

    span = na * ROWS
    row = lax.broadcasted_iota(jnp.int32, (width, width), 0)
    col = lax.broadcasted_iota(jnp.int32, (width, width), 1)
    order = (col == (row % sub) * n_chan + row // sub).astype(jnp.float32).astype(jnp.bfloat16)

    @pl.loop(0, up2_ref.shape[0] // width)
    def _(t):
        rows = pl.ds(pl.multiple_of(t * width, width), width)
        up2p[rows, :] = dot_t(up2_ref[rows, :], order).astype(jnp.bfloat16)

    down2p[...] = dot_t(down2_ref[...], order).astype(jnp.bfloat16)

    e_row = lax.broadcasted_iota(jnp.int32, (na, span), 0)
    e_col = lax.broadcasted_iota(jnp.int32, (na, span), 1)
    expand = (e_col // ROWS == e_row).astype(jnp.float32).astype(jnp.bfloat16)
    s_row = lax.broadcasted_iota(jnp.int32, (span, span), 0)
    s_col = lax.broadcasted_iota(jnp.int32, (span, span), 1)

    turn = (s_col == (s_row % ROWS) * na + s_row // ROWS).astype(jnp.float32).astype(jnp.bfloat16)

    @pl.loop(0, parts)
    def _(g):
        by_row = dot(turn, mix2_ref[g]).astype(jnp.bfloat16)
        wide = dot(by_row, expand)
        spread[g] = jnp.where(s_row % ROWS == s_col % ROWS, wide, 0.0).astype(jnp.bfloat16)

    for load in loads[2:]:
        load.wait()

    def run_second(q):
        await_first(q, fwd_recv)
        part = gathered[q].reshape(span, width)
        got = dot(spread[lax.rem(q, parts)], part).astype(jnp.bfloat16)
        second[q] = got.reshape(n_seq, paired, LANES, ROWS, width)

        @pl.loop(0, LANES)
        def _(lane):
            k = q * LANES + lane
            mixed[k, :, me_s] = second[q, me_s, :, lane]
            send_second(q, lane)

    def send_second(q, lane):
        k = q * LANES + lane

        @pl.loop(1, n_seq)
        def _(i):
            other = lax.rem(me_s + STRIDE * i, n_seq)
            pltpu.make_async_remote_copy(
                src_ref=second.at[q, other, :, lane],
                dst_ref=mixed.at[k, :, me_s],
                send_sem=ret_send.at[k],
                recv_sem=ret_recv.at[k],
                device_id={"seq": other},
                device_id_type=MESH,
            ).start()

    def await_second(k, sem):
        others = mixed.at[k, :, pl.ds(0, n_seq - 1)]
        pltpu.make_async_copy(others, others, sem.at[k]).wait()

    def swap(k, src, dst, send_sem, recv_sem):
        @pl.loop(1, n_chan)
        def _(i):
            other = lax.rem(me_c + i, n_chan)
            cols = pl.ds(pl.multiple_of(other * sub, sub), sub)
            pltpu.make_async_remote_copy(
                src_ref=src.at[k, :, cols],
                dst_ref=dst.at[k, :, my_sub],
                send_sem=send_sem.at[k],
                recv_sem=recv_sem.at[k],
                device_id={"chan": other},
                device_id_type=MESH,
            ).start()

        dst[k, :, my_sub] = src[k, :, my_sub]

    def await_swap(k, dst, sem):
        others = dst.at[k, :, pl.ds(0, width - sub)]
        pltpu.make_async_copy(others, others, sem.at[k]).wait()

    run_second(jnp.int32(0))

    @pl.loop(0, units + 2)
    def _(step):
        @pl.when(step < units)
        def _():
            k = step
            q, lane = lax.div(k, LANES), lax.rem(k, LANES)
            s, g = lax.div(q, parts), lax.rem(q, parts)

            @pl.when((lane == 1) & (q + AHEAD < chunks))
            def _():
                send_first(q + AHEAD)

            @pl.when((lane == 1) & (q + 1 < chunks))
            def _():
                run_second(q + 1)

            await_second(k, ret_recv)
            for pair in range(paired):
                x = x_ref[s, pair * LANES + lane, :, g].reshape(half, width).astype(jnp.float32)
                gate = jax.nn.sigmoid(scale_ref[...] * x + bias_ref[...])
                mix = mixed[k, pair].reshape(half, width).astype(jnp.float32)
                hidden[k, pair * half : (pair + 1) * half] = (x + mix * gate).astype(jnp.bfloat16)
            inner1[k] = dot_t(hidden[k], up1_ref[...]).astype(jnp.bfloat16)
            swap(k, inner1, perm1, c1_send, c1_recv)

        @pl.when((step >= 1) & (step < units + 1))
        def _():
            k = step - 1
            await_swap(k, perm1, c1_recv)
            acc[...] = jnp.zeros_like(acc)

            @pl.loop(0, up2_ref.shape[0] // width, unroll=True)
            def _(t):
                tile = pl.ds(pl.multiple_of(t * width, width), width)
                act = jax.nn.gelu(dot_t(perm1[k], up2p[tile, :]), approximate=True)
                acc[...] += dot_t(act.astype(jnp.bfloat16), down1_ref[:, tile])

            inner2[k] = acc[...].astype(jnp.bfloat16)
            swap(k, inner2, perm2, c2_send, c2_recv)

        @pl.when(step >= 2)
        def _():
            k = step - 2
            q, lane = lax.div(k, LANES), lax.rem(k, LANES)
            s, g = lax.div(q, parts), lax.rem(q, parts)
            await_swap(k, perm2, c2_recv)
            got = dot_t(perm2[k], down2p[...])
            got = (hidden[k].astype(jnp.float32) + got).astype(jnp.bfloat16)
            result[k] = got.reshape(paired, n_seq, ROWS, width)
            for pair in range(paired):
                a = pair * LANES + lane
                src, dst = result.at[k, pair], out_ref.at[s, :, g, :, my_cols]

                @pl.when(a == me_c)
                def _(src=src, dst=dst):
                    pltpu.make_async_copy(src, dst, out_local.at[s]).start()

                @pl.when(a != me_c)
                def _(src=src, dst=dst, a=a):
                    pltpu.make_async_remote_copy(
                        src_ref=src,
                        dst_ref=dst,
                        send_sem=out_send.at[s],
                        recv_sem=out_recv.at[s],
                        device_id={"chan": a},
                        device_id_type=MESH,
                    ).start()

    @pl.loop(0, seqs)
    def _(s):
        landed = out_ref.at[s, :, :, :, pl.ds(0, width * (n_chan - 1))]
        pltpu.make_async_copy(landed, landed, out_send.at[s]).wait()
        pltpu.make_async_copy(landed, landed, out_recv.at[s]).wait()
        one = out_ref.at[s, :, :, :, pl.ds(0, width)]
        pltpu.make_async_copy(one, one, out_local.at[s]).wait()

    @pl.loop(0, chunks)
    def _(q):
        await_first(q, fwd_send)

    @pl.loop(0, units)
    def _(k):
        await_second(k, ret_send)
        await_swap(k, perm1, c1_send)
        await_swap(k, perm2, c2_send)


def copy_kernel(src_ref, dst_ref):
    dst_ref[...] = src_ref[...]


def hand_over(array):
    seqs, rows, width = array.shape
    block = pl.BlockSpec((1, rows // 2, width), lambda s, i: (s, i, 0))
    return pl.pallas_call(
        copy_kernel,
        out_shape=jax.ShapeDtypeStruct(array.shape, array.dtype),
        grid=(seqs, 2),
        in_specs=[block],
        out_specs=block,
    )(array)


def fused_layer(
    inputs,
    mix_first,
    mix_second,
    gate_scale,
    gate_bias,
    up_first,
    up_second,
    down_first,
    down_second,
):
    n_seq, n_chan = lax.axis_size("seq"), lax.axis_size("chan")
    seqs, rows, width = inputs.shape
    blocks, group = mix_first.shape[0], mix_first.shape[1]
    own_b, na = mix_second.shape[0], mix_second.shape[1]
    parts = own_b // ROWS
    chunks = seqs * parts
    units = chunks * LANES
    paired = blocks // LANES
    bf = jnp.bfloat16
    per_unit = pltpu.VMEM((units, paired * n_seq * ROWS, width), bf)
    by_device = pltpu.VMEM((units, paired, n_seq, ROWS, width), bf)
    dma = pltpu.SemaphoreType.DMA
    out = pl.pallas_call(
        functools.partial(layer_kernel, n_seq, n_chan),
        out_shape=jax.ShapeDtypeStruct((seqs, n_seq, parts, ROWS, width * n_chan), bf),
        in_specs=[pl.BlockSpec(memory_space=pltpu.VMEM)] * 5
        + [pl.BlockSpec(memory_space=pl.ANY)] * 4,
        out_specs=pl.BlockSpec(memory_space=pl.ANY),
        scratch_shapes=[
            pltpu.VMEM((seqs, blocks, n_seq, parts, ROWS, width), bf),
            pltpu.VMEM((chunks, na, ROWS, width), bf),
            pltpu.VMEM((chunks, n_seq, paired, LANES, ROWS, width), bf),
            by_device,
            per_unit,
            per_unit,
            per_unit,
            per_unit,
            per_unit,
            by_device,
            pltpu.VMEM(up_second.shape[1:], bf),
            pltpu.VMEM(down_second.shape[1:], bf),
            pltpu.VMEM((parts, na * ROWS, na * ROWS), bf),
            pltpu.VMEM((paired * n_seq * ROWS, width), jnp.float32),
            pltpu.VMEM(up_first.shape[1:], bf),
            pltpu.VMEM(up_second.shape[1:], bf),
            pltpu.VMEM(down_first.shape[1:], bf),
            pltpu.VMEM(down_second.shape[1:], bf),
            dma((4,)),
            dma((chunks,)),
            dma((chunks,)),
            dma((units,)),
            dma((units,)),
            dma((units,)),
            dma((units,)),
            dma((units,)),
            dma((units,)),
            dma((seqs,)),
            dma((seqs,)),
            dma((seqs,)),
        ],
        compiler_params=pltpu.CompilerParams(
            collective_id=0, has_side_effects=True, vmem_limit_bytes=56 * 1024 * 1024
        ),
    )(
        inputs.reshape(seqs, blocks, n_seq, parts, ROWS, width),
        mix_first,
        mix_second.reshape(parts, ROWS * na, na),
        gate_scale.reshape(1, width),
        gate_bias.reshape(1, width),
        up_first[0],
        up_second[0],
        down_first[0],
        down_second[0],
    )
    return hand_over(out.reshape(seqs, group, width * n_chan))


def on_device(inputs, mix_first, mix_second, *rest):
    blocks = mix_first.shape[0]
    whole = mix_second.shape[0] % ROWS == 0 and blocks % LANES == 0
    fits = whole and blocks == lax.axis_size("chan") and lax.axis_size("seq") % STRIDE != 0
    run = fused_layer if fits else plain_layer
    return run(inputs, mix_first, mix_second, *rest)


def plain_layer(
    inputs,
    mix_first,
    mix_second,
    gate_scale,
    gate_bias,
    up_first,
    up_second,
    down_first,
    down_second,
):
    seq_count, row_count, chan_width = inputs.shape
    blocks_here = mix_first.shape[0]
    group_width = mix_first.shape[1]
    grouped = inputs.reshape(seq_count, blocks_here, group_width, chan_width)
    first_pass = jnp.einsum(
        "abq,saqc->sabc", mix_first, grouped, preferred_element_type=jnp.float32
    ).astype(jnp.bfloat16)
    mixed_rows = jnp.einsum(
        "bxy,sybc->sxbc",
        mix_second,
        lax.all_to_all(first_pass, "seq", split_axis=2, concat_axis=1, tiled=True),
        preferred_element_type=jnp.float32,
    ).astype(jnp.bfloat16)
    restored = lax.all_to_all(mixed_rows, "seq", split_axis=1, concat_axis=2, tiled=True).reshape(
        seq_count, row_count, chan_width
    )
    residual_in = inputs.astype(jnp.float32)
    hidden = (
        residual_in
        + restored.astype(jnp.float32) * jax.nn.sigmoid(gate_scale * residual_in + gate_bias)
    ).astype(jnp.bfloat16)
    expanded = shard_monarch(hidden, up_first, up_second)
    activated = jax.nn.gelu(expanded, approximate=True).astype(jnp.bfloat16)
    contracted = shard_monarch(activated, down_first, down_second)
    result = (hidden.astype(jnp.float32) + contracted).astype(jnp.bfloat16)
    return lax.all_to_all(result, "chan", split_axis=1, concat_axis=2, tiled=True)


def solution(mesh):
    return jax.shard_map(
        on_device,
        mesh=mesh,
        in_specs=(
            P(None, "seq", "chan"),
            P("seq", None, None),
            P("seq", None, None),
            P("chan"),
            P("chan"),
            P("chan", None, None),
            P("chan", None, None),
            P("chan", None, None),
            P("chan", None, None),
        ),
        out_specs=P(None, ("seq", "chan"), None),
        check_vma=False,
    )
```

```python
import functools

import jax
import jax.numpy as jnp
from jax import lax
from jax.experimental import pallas as pl
from jax.experimental.pallas import tpu as pltpu
from jax.sharding import PartitionSpec as P

MESH = pl.DeviceIdType.MESH
ROWS = 16
LANES = 2
AHEAD = 2
STRIDE = 3


def shard_monarch(values, inner_weight, outer_weight):
    chan_count = lax.axis_size("chan")
    inner_width = inner_weight.shape[1]
    out_width = outer_weight.shape[1]
    sub_width = inner_width // chan_count
    seq_count, row_count = (values.shape[0], values.shape[1])
    inner_rows = jnp.einsum(
        "qp,stp->stq", inner_weight[0], values, preferred_element_type=jnp.float32
    )
    inner_rows = inner_rows.astype(jnp.bfloat16).reshape(
        seq_count, row_count, chan_count, sub_width
    )
    permuted = lax.all_to_all(inner_rows, "chan", split_axis=2, concat_axis=2, tiled=True)
    outer_blocks = outer_weight[0].reshape(out_width, sub_width, chan_count)
    return jnp.einsum("oqc,stcq->sto", outer_blocks, permuted, preferred_element_type=jnp.float32)


def dot(a, b):
    return jnp.dot(a, b, preferred_element_type=jnp.float32)


def dot_t(a, b):
    return lax.dot_general(a, b, (((1,), (1,)), ((), ())), preferred_element_type=jnp.float32)


def layer_kernel(
    n_seq,
    n_chan,
    x_ref,
    mix1_ref,
    mix2_ref,
    scale_ref,
    bias_ref,
    up1_hbm,
    up2_hbm,
    down1_hbm,
    down2_hbm,
    out_ref,
    first,
    gathered,
    second,
    mixed,
    hidden,
    inner1,
    perm1,
    inner2,
    perm2,
    result,
    up2p,
    down2p,
    spread,
    acc,
    up1_ref,
    up2_ref,
    down1_ref,
    down2_ref,
    load_sem,
    fwd_send,
    fwd_recv,
    ret_send,
    ret_recv,
    c1_send,
    c1_recv,
    c2_send,
    c2_recv,
    out_send,
    out_recv,
    out_local,
):
    seqs, blocks, _, parts, _, width = x_ref.shape
    na = n_seq * blocks
    group = n_seq * parts * ROWS
    sub = width // n_chan
    chunks = seqs * parts
    units = chunks * LANES
    paired = blocks // LANES
    half = n_seq * ROWS
    me_s = lax.axis_index("seq")
    me_c = lax.axis_index("chan")

    barrier = pltpu.get_barrier_semaphore()
    for i in range(1, n_seq):
        pl.semaphore_signal(
            barrier, inc=1, device_id={"seq": lax.rem(me_s + i, n_seq)}, device_id_type=MESH
        )
    for i in range(1, n_chan):
        pl.semaphore_signal(
            barrier, inc=1, device_id={"chan": lax.rem(me_c + i, n_chan)}, device_id_type=MESH
        )

    loads = [
        pltpu.make_async_copy(src, dst, load_sem.at[i])
        for i, (src, dst) in enumerate(
            [(up2_hbm, up2_ref), (down2_hbm, down2_ref), (up1_hbm, up1_ref), (down1_hbm, down1_ref)]
        )
    ]
    for load in loads:
        load.start()

    my_a = pl.ds(me_s * blocks, blocks)
    my_sub = pl.ds(pl.multiple_of(me_c * sub, sub), sub)
    my_cols = pl.ds(pl.multiple_of(me_c * width, width), width)

    def run_first(s):
        @pl.loop(0, blocks)
        def _(a):
            got = dot(mix1_ref[a], x_ref[s, a].reshape(group, width)).astype(jnp.bfloat16)
            first[s, a] = got.reshape(n_seq, parts, ROWS, width)

        for g in range(parts):
            gathered[s * parts + g, my_a] = first[s, :, me_s, g]

    def send_first(q):
        @pl.loop(1, n_seq)
        def _(i):
            other = lax.rem(me_s + STRIDE * i, n_seq)
            pltpu.make_async_remote_copy(
                src_ref=first.at[lax.div(q, parts), :, other, lax.rem(q, parts)],
                dst_ref=gathered.at[q, my_a],
                send_sem=fwd_send.at[q],
                recv_sem=fwd_recv.at[q],
                device_id={"seq": other},
                device_id_type=MESH,
            ).start()

    def await_first(q, sem):
        others = gathered.at[q, pl.ds(0, na - blocks)]
        pltpu.make_async_copy(others, others, sem.at[q]).wait()

    run_first(0)
    pl.semaphore_wait(barrier, n_seq + n_chan - 2)
    for q in range(min(AHEAD, parts)):
        send_first(jnp.int32(q))

    @pl.loop(1, seqs)
    def _(s):
        run_first(s)

    for load in loads[:2]:
        load.wait()

    span = na * ROWS
    row = lax.broadcasted_iota(jnp.int32, (width, width), 0)
    col = lax.broadcasted_iota(jnp.int32, (width, width), 1)
    order = (col == (row % sub) * n_chan + row // sub).astype(jnp.float32).astype(jnp.bfloat16)

    @pl.loop(0, up2_ref.shape[0] // width)
    def _(t):
        rows = pl.ds(pl.multiple_of(t * width, width), width)
        up2p[rows, :] = dot_t(up2_ref[rows, :], order).astype(jnp.bfloat16)

    down2p[...] = dot_t(down2_ref[...], order).astype(jnp.bfloat16)

    e_row = lax.broadcasted_iota(jnp.int32, (na, span), 0)
    e_col = lax.broadcasted_iota(jnp.int32, (na, span), 1)
    expand = (e_col // ROWS == e_row).astype(jnp.float32).astype(jnp.bfloat16)
    s_row = lax.broadcasted_iota(jnp.int32, (span, span), 0)
    s_col = lax.broadcasted_iota(jnp.int32, (span, span), 1)

    turn = (s_col == (s_row % ROWS) * na + s_row // ROWS).astype(jnp.float32).astype(jnp.bfloat16)

    @pl.loop(0, parts)
    def _(g):
        by_row = dot(turn, mix2_ref[g]).astype(jnp.bfloat16)
        wide = dot(by_row, expand)
        spread[g] = jnp.where(s_row % ROWS == s_col % ROWS, wide, 0.0).astype(jnp.bfloat16)

    for load in loads[2:]:
        load.wait()

    def run_second(q):
        await_first(q, fwd_recv)
        part = gathered[q].reshape(span, width)
        got = dot(spread[lax.rem(q, parts)], part).astype(jnp.bfloat16)
        second[q] = got.reshape(n_seq, paired, LANES, ROWS, width)

        @pl.loop(0, LANES)
        def _(lane):
            k = q * LANES + lane
            mixed[k, :, me_s] = second[q, me_s, :, lane]
            send_second(q, lane)

    def send_second(q, lane):
        k = q * LANES + lane

        @pl.loop(1, n_seq)
        def _(i):
            other = lax.rem(me_s + STRIDE * i, n_seq)
            pltpu.make_async_remote_copy(
                src_ref=second.at[q, other, :, lane],
                dst_ref=mixed.at[k, :, me_s],
                send_sem=ret_send.at[k],
                recv_sem=ret_recv.at[k],
                device_id={"seq": other},
                device_id_type=MESH,
            ).start()

    def await_second(k, sem):
        others = mixed.at[k, :, pl.ds(0, n_seq - 1)]
        pltpu.make_async_copy(others, others, sem.at[k]).wait()

    def swap(k, src, dst, send_sem, recv_sem):
        @pl.loop(1, n_chan)
        def _(i):
            other = lax.rem(me_c + i, n_chan)
            cols = pl.ds(pl.multiple_of(other * sub, sub), sub)
            pltpu.make_async_remote_copy(
                src_ref=src.at[k, :, cols],
                dst_ref=dst.at[k, :, my_sub],
                send_sem=send_sem.at[k],
                recv_sem=recv_sem.at[k],
                device_id={"chan": other},
                device_id_type=MESH,
            ).start()

        dst[k, :, my_sub] = src[k, :, my_sub]

    def await_swap(k, dst, sem):
        others = dst.at[k, :, pl.ds(0, width - sub)]
        pltpu.make_async_copy(others, others, sem.at[k]).wait()

    run_second(jnp.int32(0))

    @pl.loop(0, units + 2)
    def _(step):
        @pl.when(step < units)
        def _():
            k = step
            q, lane = lax.div(k, LANES), lax.rem(k, LANES)
            s, g = lax.div(q, parts), lax.rem(q, parts)

            @pl.when((lane == 1) & (q + AHEAD < chunks))
            def _():
                send_first(q + AHEAD)

            @pl.when((lane == 1) & (q + 1 < chunks))
            def _():
                run_second(q + 1)

            await_second(k, ret_recv)
            for pair in range(paired):
                x = x_ref[s, pair * LANES + lane, :, g].reshape(half, width).astype(jnp.float32)
                gate = jax.nn.sigmoid(scale_ref[...] * x + bias_ref[...])
                mix = mixed[k, pair].reshape(half, width).astype(jnp.float32)
                hidden[k, pair * half : (pair + 1) * half] = (x + mix * gate).astype(jnp.bfloat16)
            inner1[k] = dot_t(hidden[k], up1_ref[...]).astype(jnp.bfloat16)
            swap(k, inner1, perm1, c1_send, c1_recv)

        @pl.when((step >= 1) & (step < units + 1))
        def _():
            k = step - 1
            await_swap(k, perm1, c1_recv)
            acc[...] = jnp.zeros_like(acc)

            @pl.loop(0, up2_ref.shape[0] // width, unroll=True)
            def _(t):
                tile = pl.ds(pl.multiple_of(t * width, width), width)
                act = jax.nn.gelu(dot_t(perm1[k], up2p[tile, :]), approximate=True)
                acc[...] += dot_t(act.astype(jnp.bfloat16), down1_ref[:, tile])

            inner2[k] = acc[...].astype(jnp.bfloat16)
            swap(k, inner2, perm2, c2_send, c2_recv)

        @pl.when(step >= 2)
        def _():
            k = step - 2
            q, lane = lax.div(k, LANES), lax.rem(k, LANES)
            s, g = lax.div(q, parts), lax.rem(q, parts)
            await_swap(k, perm2, c2_recv)
            got = dot_t(perm2[k], down2p[...])
            got = (hidden[k].astype(jnp.float32) + got).astype(jnp.bfloat16)
            result[k] = got.reshape(paired, n_seq, ROWS, width)
            for pair in range(paired):
                a = pair * LANES + lane
                src, dst = result.at[k, pair], out_ref.at[s, :, g, :, my_cols]

                @pl.when(a == me_c)
                def _(src=src, dst=dst):
                    pltpu.make_async_copy(src, dst, out_local.at[s]).start()

                @pl.when(a != me_c)
                def _(src=src, dst=dst, a=a):
                    pltpu.make_async_remote_copy(
                        src_ref=src,
                        dst_ref=dst,
                        send_sem=out_send.at[s],
                        recv_sem=out_recv.at[s],
                        device_id={"chan": a},
                        device_id_type=MESH,
                    ).start()

    @pl.loop(0, seqs)
    def _(s):
        landed = out_ref.at[s, :, :, :, pl.ds(0, width * (n_chan - 1))]
        pltpu.make_async_copy(landed, landed, out_send.at[s]).wait()
        pltpu.make_async_copy(landed, landed, out_recv.at[s]).wait()
        one = out_ref.at[s, :, :, :, pl.ds(0, width)]
        pltpu.make_async_copy(one, one, out_local.at[s]).wait()

    @pl.loop(0, chunks)
    def _(q):
        await_first(q, fwd_send)

    @pl.loop(0, units)
    def _(k):
        await_second(k, ret_send)
        await_swap(k, perm1, c1_send)
        await_swap(k, perm2, c2_send)


def fused_layer(
    inputs,
    mix_first,
    mix_second,
    gate_scale,
    gate_bias,
    up_first,
    up_second,
    down_first,
    down_second,
):
    n_seq, n_chan = lax.axis_size("seq"), lax.axis_size("chan")
    seqs, rows, width = inputs.shape
    blocks, group = mix_first.shape[0], mix_first.shape[1]
    own_b, na = mix_second.shape[0], mix_second.shape[1]
    parts = own_b // ROWS
    chunks = seqs * parts
    units = chunks * LANES
    paired = blocks // LANES
    bf = jnp.bfloat16
    per_unit = pltpu.VMEM((units, paired * n_seq * ROWS, width), bf)
    by_device = pltpu.VMEM((units, paired, n_seq, ROWS, width), bf)
    dma = pltpu.SemaphoreType.DMA
    out = pl.pallas_call(
        functools.partial(layer_kernel, n_seq, n_chan),
        out_shape=jax.ShapeDtypeStruct((seqs, n_seq, parts, ROWS, width * n_chan), bf),
        in_specs=[pl.BlockSpec(memory_space=pltpu.VMEM)] * 5
        + [pl.BlockSpec(memory_space=pl.ANY)] * 4,
        out_specs=pl.BlockSpec(memory_space=pl.ANY),
        scratch_shapes=[
            pltpu.VMEM((seqs, blocks, n_seq, parts, ROWS, width), bf),
            pltpu.VMEM((chunks, na, ROWS, width), bf),
            pltpu.VMEM((chunks, n_seq, paired, LANES, ROWS, width), bf),
            by_device,
            per_unit,
            per_unit,
            per_unit,
            per_unit,
            per_unit,
            by_device,
            pltpu.VMEM(up_second.shape[1:], bf),
            pltpu.VMEM(down_second.shape[1:], bf),
            pltpu.VMEM((parts, na * ROWS, na * ROWS), bf),
            pltpu.VMEM((paired * n_seq * ROWS, width), jnp.float32),
            pltpu.VMEM(up_first.shape[1:], bf),
            pltpu.VMEM(up_second.shape[1:], bf),
            pltpu.VMEM(down_first.shape[1:], bf),
            pltpu.VMEM(down_second.shape[1:], bf),
            dma((4,)),
            dma((chunks,)),
            dma((chunks,)),
            dma((units,)),
            dma((units,)),
            dma((units,)),
            dma((units,)),
            dma((units,)),
            dma((units,)),
            dma((seqs,)),
            dma((seqs,)),
            dma((seqs,)),
        ],
        compiler_params=pltpu.CompilerParams(
            collective_id=0, has_side_effects=True, vmem_limit_bytes=56 * 1024 * 1024
        ),
    )(
        inputs.reshape(seqs, blocks, n_seq, parts, ROWS, width),
        mix_first,
        mix_second.reshape(parts, ROWS * na, na),
        gate_scale.reshape(1, width),
        gate_bias.reshape(1, width),
        up_first[0],
        up_second[0],
        down_first[0],
        down_second[0],
    )
    return out.reshape(seqs, group, width * n_chan)


def on_device(inputs, mix_first, mix_second, *rest):
    blocks = mix_first.shape[0]
    whole = mix_second.shape[0] % ROWS == 0 and blocks % LANES == 0
    fits = whole and blocks == lax.axis_size("chan") and lax.axis_size("seq") % STRIDE != 0
    run = fused_layer if fits else plain_layer
    return run(inputs, mix_first, mix_second, *rest)


def plain_layer(
    inputs,
    mix_first,
    mix_second,
    gate_scale,
    gate_bias,
    up_first,
    up_second,
    down_first,
    down_second,
):
    seq_count, row_count, chan_width = inputs.shape
    blocks_here = mix_first.shape[0]
    group_width = mix_first.shape[1]
    grouped = inputs.reshape(seq_count, blocks_here, group_width, chan_width)
    first_pass = jnp.einsum(
        "abq,saqc->sabc", mix_first, grouped, preferred_element_type=jnp.float32
    ).astype(jnp.bfloat16)
    mixed_rows = jnp.einsum(
        "bxy,sybc->sxbc",
        mix_second,
        lax.all_to_all(first_pass, "seq", split_axis=2, concat_axis=1, tiled=True),
        preferred_element_type=jnp.float32,
    ).astype(jnp.bfloat16)
    restored = lax.all_to_all(mixed_rows, "seq", split_axis=1, concat_axis=2, tiled=True).reshape(
        seq_count, row_count, chan_width
    )
    residual_in = inputs.astype(jnp.float32)
    hidden = (
        residual_in
        + restored.astype(jnp.float32) * jax.nn.sigmoid(gate_scale * residual_in + gate_bias)
    ).astype(jnp.bfloat16)
    expanded = shard_monarch(hidden, up_first, up_second)
    activated = jax.nn.gelu(expanded, approximate=True).astype(jnp.bfloat16)
    contracted = shard_monarch(activated, down_first, down_second)
    result = (hidden.astype(jnp.float32) + contracted).astype(jnp.bfloat16)
    return lax.all_to_all(result, "chan", split_axis=1, concat_axis=2, tiled=True)


def solution(mesh):
    return jax.shard_map(
        on_device,
        mesh=mesh,
        in_specs=(
            P(None, "seq", "chan"),
            P("seq", None, None),
            P("seq", None, None),
            P("chan"),
            P("chan"),
            P("chan", None, None),
            P("chan", None, None),
            P("chan", None, None),
            P("chan", None, None),
        ),
        out_specs=P(None, ("seq", "chan"), None),
        check_vma=False,
    )
```
